256 devices in a mesh: dp: 32 (over x, y, core), ctx: 8 (over z).
Axes of the slice: x: 4, y: 4, z: 8, core: 2. Of those that a mesh axis runs over, the one named last changes fastest.
Arguments:
- queries: bfloat16 [32768, 2048], P(('dp', 'ctx')), may hold values from -5 to 5
- keys: bfloat16 [32768, 2048], P(('dp', 'ctx')), may hold values from -5 to 5
- values: bfloat16 [32768, 2048], P(('dp', 'ctx')), may hold values from -6 to 6
- grad_out: bfloat16 [32768, 2048], P(('dp', 'ctx')), may hold values from -6 to 6
- doc_ids: int32 [32768], replicated, may hold values from 0 to 32512, as said below
- tile_pairs: int32 [768, 2], replicated, may hold values from -1 to 255, as said below
Outputs:
- attended: bfloat16 [32768, 2048], P(('dp', 'ctx'))
- grad_q: bfloat16 [32768, 2048], P(('dp', 'ctx'))
- grad_k: bfloat16 [32768, 2048], P(('dp', 'ctx'))
- grad_v: bfloat16 [32768, 2048], P(('dp', 'ctx'))
The draws below stay inside these ranges and needn't reach their ends.
Inputs may be any that keep to these rules, and one draw needn't show every extreme that they name: `doc_ids`: documents lie end to end, so ids never fall; no document holds more than 256 tokens; all but the batch's last two hold 64 to 256 tokens, some exactly 256; the last document begins at token 32512. `tile_pairs`: each used row holds an owner tile and a partner tile no lower than it; the used rows are exactly the pairs of tiles that hold tokens of one common document, each pair once, in no particular order; the other rows hold -1 in both columns.
All inputs are finite; a program needn't handle non-finite values.
Results may differ from the reference program's by a relative error of at most 0.029.
Values may be sent and summed in bfloat16 or wider, within the bound.
A program may use at most 128 MiB of HBM per device.

```python
import math
import jax
import jax.numpy as jnp
from jax import lax

H = 16
HEAD = 128
TILE = 128
TOK_DEV = 128
HD = 2048
REACH = 256
TOKENS = 32768


def documents(key):
    number = TOKENS // (REACH // 4) + 1
    lengths = jax.random.randint(jax.random.fold_in(key, 21), (number,), REACH // 4, REACH + 1, dtype=jnp.int32)
    lengths = lengths.at[0].set(REACH)
    ends = jnp.cumsum(lengths).astype(jnp.int32)
    starts = (ends - lengths).astype(jnp.int32)
    positions = jnp.arange(TOKENS, dtype=jnp.int32)
    which = jnp.searchsorted(ends, positions, side='right')
    firsts = starts[which].astype(jnp.int32)
    last_start = jnp.int32(TOKENS - REACH)
    return jnp.where(positions >= last_start, last_start, firsts).astype(jnp.int32)


def draw_queries(key, part):
    key = jax.random.fold_in(key, 1)
    field = jnp.clip(jax.random.normal(key, (TOKENS, H * HEAD), jnp.float32), -5.0, 5.0)
    return field.astype(jnp.bfloat16)


def draw_keys(key, part):
    key = jax.random.fold_in(key, 2)
    field = jnp.clip(jax.random.normal(key, (TOKENS, H * HEAD), jnp.float32), -5.0, 5.0)
    return field.astype(jnp.bfloat16)


def draw_doc_ids(key, part):
    firsts = documents(key)
    return firsts


def draw_tile_pairs(key, part):
    firsts = documents(key)
    key = jax.random.fold_in(key, 4)
    count_tiles = TOKENS // TILE
    offsets_all = REACH // TILE + 1
    owner = jnp.repeat(jnp.arange(count_tiles, dtype=jnp.int32), offsets_all)
    offset = jnp.tile(jnp.arange(offsets_all, dtype=jnp.int32), count_tiles)
    partner = owner + offset
    inside = partner < count_tiles
    last_of = firsts[(owner + 1) * TILE - 1]
    first_of = firsts[jnp.minimum(partner, count_tiles - 1) * TILE]
    present = (offset == 0) | inside & (last_of == first_of)
    table = jnp.stack([jnp.where(present, owner, -1), jnp.where(present, partner, -1)], axis=1)
    order = jax.random.permutation(key, table.shape[0])
    return table[order].astype(jnp.int32)


def block_scale(own_key, dims, shards, least, high):
    loudness = 1.0
    for axis_at, blocks in shards:
        heights = jax.random.uniform(jax.random.fold_in(jax.random.fold_in(own_key, 6), axis_at), (blocks,), jnp.float32, least / len(shards), high / len(shards))
        loudness = loudness * jnp.repeat(jnp.exp(heights), dims[axis_at] // blocks).reshape((-1,) + (1,) * (len(dims) - 1 - axis_at))
    return loudness


def noise(own_key, dims, deviation, bound, cuts=(), kind=jnp.bfloat16):
    entries = deviation * jax.random.normal(own_key, dims, jnp.float32)
    if cuts:
        entries = entries * block_scale(own_key, dims, cuts, -0.22, 0.18)
    return jnp.clip(entries, -bound, bound).astype(kind)


def setup_inputs(seed: int = 0) -> dict:
    arg_keys = jax.random.split(jax.random.key(seed), 7)
    return {
        "queries": draw_queries(jax.random.fold_in(arg_keys[6], 71), 0),
        "keys": draw_keys(jax.random.fold_in(arg_keys[6], 71), 0),
        "values": noise(arg_keys[2], (TOKENS, HD), 1.0, 6.0, ((0, 256),)),
        "grad_out": noise(arg_keys[3], (TOKENS, HD), 1.0, 6.0, ((0, 256),)),
        "doc_ids": draw_doc_ids(jax.random.fold_in(arg_keys[6], 71), 0),
        "tile_pairs": draw_tile_pairs(jax.random.fold_in(arg_keys[6], 71), 0),
    }


def rounded(array):
    low = lax.optimization_barrier(array.astype(jnp.bfloat16))
    return low.astype(jnp.float32)

def listed(pairs, first_tiles, second_tiles):
    owner = pairs[:, 0][:, None, None]
    partner = pairs[:, 1][:, None, None]
    first = first_tiles[None, :, None]
    second = second_tiles[None, None, :]
    found = (owner == first) & (partner == second) | (owner == second) & (partner == first)
    return jnp.any(found, axis=0)

def token_mask(pairs, first_ids, second_ids, first_start, second_start, first_count, second_count):
    first_tiles = first_start // TILE + jnp.arange(first_count // TILE, dtype=jnp.int32)
    second_tiles = second_start // TILE + jnp.arange(second_count // TILE, dtype=jnp.int32)
    tiled = listed(pairs, first_tiles, second_tiles)
    spread = jnp.repeat(jnp.repeat(tiled, TILE, axis=0), TILE, axis=1)
    return spread & (first_ids[:, None] == second_ids[None, :])

def masked_scores(left, right, mask, scale):
    scores = jnp.einsum('agd,bgd->gab', left, right) * scale
    return jnp.where(mask[None], scores, -jnp.inf)

def reference(queries, keys, values, grad_out, doc_ids, tile_pairs):
    scale = 1.0 / math.sqrt(HEAD)
    width = H * HEAD
    window = TOK_DEV + 2 * REACH
    blocks = TOKENS // TOK_DEV
    zero_rows = jnp.zeros((REACH, width), jnp.bfloat16)
    filler = -jnp.ones((REACH,), jnp.int32)
    pad_ids = jnp.concatenate([filler, doc_ids, filler])
    pad_keys = jnp.concatenate([zero_rows, keys, zero_rows])
    pad_values = jnp.concatenate([zero_rows, values, zero_rows])
    pad_queries = jnp.concatenate([zero_rows, queries, zero_rows])
    pad_grads = jnp.concatenate([zero_rows, grad_out, zero_rows])

    def cut(array, start, number):
        piece = lax.dynamic_slice_in_dim(array, start, number, 0)
        return piece.astype(jnp.float32).reshape(number, H, HEAD)

    def forward_block(block):
        start = (block * TOK_DEV).astype(jnp.int32)
        query = cut(queries, start, TOK_DEV)
        grads = cut(grad_out, start, TOK_DEV)
        near_keys = cut(pad_keys, start, window)
        near_values = cut(pad_values, start, window)
        own_ids = lax.dynamic_slice_in_dim(doc_ids, start, TOK_DEV, 0)
        near_ids = lax.dynamic_slice_in_dim(pad_ids, start, window, 0)
        mask = token_mask(tile_pairs, own_ids, near_ids, start, start - REACH, TOK_DEV, window)
        scores = masked_scores(query, near_keys, mask, scale)
        top = lax.optimization_barrier(jnp.max(scores, axis=2, keepdims=True))
        lse = top[:, :, 0] + jnp.log(lax.optimization_barrier(jnp.sum(jnp.exp(scores - top), axis=2)))
        probs = jnp.exp(scores - lse[:, :, None])
        probs_low = rounded(probs)
        attended = jnp.einsum('gab,bgd->agd', probs_low, near_values).astype(jnp.bfloat16)
        delta = lax.optimization_barrier(jnp.sum(grads * attended.astype(jnp.float32), axis=2)).T
        dprobs = jnp.einsum('agd,bgd->gab', grads, near_values)
        dscores = rounded(probs * (dprobs - delta[:, :, None]))
        grad_q = (jnp.einsum('gab,bgd->agd', dscores, near_keys) * scale).astype(jnp.bfloat16)
        return (attended.reshape(TOK_DEV, width), grad_q.reshape(TOK_DEV, width), lse.T, delta.T)
    attended, grad_q, lse, delta = lax.map(forward_block, jnp.arange(blocks, dtype=jnp.int32))
    zero_stats = jnp.zeros((REACH, H), jnp.float32)
    pad_lse = jnp.concatenate([zero_stats, lse.reshape(TOKENS, H), zero_stats])
    pad_delta = jnp.concatenate([zero_stats, delta.reshape(TOKENS, H), zero_stats])

    def backward_block(block):
        start = (block * TOK_DEV).astype(jnp.int32)
        own_keys = cut(keys, start, TOK_DEV)
        own_values = cut(values, start, TOK_DEV)
        near_queries = cut(pad_queries, start, window)
        near_grads = cut(pad_grads, start, window)
        near_lse = lax.dynamic_slice_in_dim(pad_lse, start, window, 0)
        near_delta = lax.dynamic_slice_in_dim(pad_delta, start, window, 0)
        own_ids = lax.dynamic_slice_in_dim(doc_ids, start, TOK_DEV, 0)
        near_ids = lax.dynamic_slice_in_dim(pad_ids, start, window, 0)
        mask = token_mask(tile_pairs, near_ids, own_ids, start - REACH, start, window, TOK_DEV)
        scores = masked_scores(near_queries, own_keys, mask, scale)
        probs = jnp.exp(scores - near_lse.T[:, :, None])
        probs_low = rounded(probs)
        dprobs = jnp.einsum('wgd,tgd->gwt', near_grads, own_values)
        dscores = rounded(probs * (dprobs - near_delta.T[:, :, None]))
        grad_k = (jnp.einsum('gwt,wgd->tgd', dscores, near_queries) * scale).astype(jnp.bfloat16)
        grad_v = jnp.einsum('gwt,wgd->tgd', probs_low, near_grads).astype(jnp.bfloat16)
        return (grad_k.reshape(TOK_DEV, width), grad_v.reshape(TOK_DEV, width))
    grad_k, grad_v = lax.map(backward_block, jnp.arange(blocks, dtype=jnp.int32))
    return (attended.reshape(TOKENS, width), grad_q.reshape(TOKENS, width), grad_k.reshape(TOKENS, width), grad_v.reshape(TOKENS, width))
```

```python
import functools
import math

import jax
import jax.numpy as jnp
from jax import lax
from jax.experimental import pallas as pl
from jax.experimental.pallas import tpu as pltpu
from jax.sharding import PartitionSpec as P

HEAD = 128
TILE = 128
HALF = 8
PER = 2
GROUPS = HALF // PER
WIDE = PER * HEAD
SPLIT = HALF * HEAD
SCALE = 1.0 / math.sqrt(HEAD)
LOG2E = math.log2(math.e)
FAR = -1e30
MESH_ID = pl.DeviceIdType.MESH


def dot_nt(a, b):
    return lax.dot_general(a, b, (((1,), (1,)), ((), ())), preferred_element_type=jnp.float32)


def dot_nn(a, b):
    return lax.dot_general(a, b, (((1,), (0,)), ((), ())), preferred_element_type=jnp.float32)


def dot_tn(a, b):
    return lax.dot_general(a, b, (((0,), (0,)), ((), ())), preferred_element_type=jnp.float32)


def columns(start, size):
    return pl.ds(pl.multiple_of(start, HEAD), size)


def kernel(
    n_dp, n_ctx,
    q_ref, k_ref, v_ref, g_ref, ids_ref, pairs_ref,
    att_ref, gq_ref, gk_ref, gv_ref,
    own, near, stage, result, late, done, bias_a, bias_b,
    own_sem, e1_send, e1_recv, e2_send, e2_recv, late_send, late_recv, out_sem,
):
    n = n_dp * n_ctx
    me = lax.axis_index("dp") * n_ctx + lax.axis_index("ctx")
    right = lax.rem(me + 1, n)
    left = lax.rem(me + n - 1, n)
    target = [(x // n_ctx, lax.rem(x, n_ctx)) for x in (right, left)]
    inputs = (q_ref, k_ref, v_ref, g_ref)
    outputs = (att_ref, gq_ref, gk_ref, gv_ref)

    def own_copy(a):
        return pltpu.make_async_copy(inputs[a], own.at[a], own_sem.at[a])

    def first(d, g, a):
        cols = columns(g * WIDE, WIDE)
        return pltpu.make_async_remote_copy(
            src_ref=inputs[a].at[:, cols], dst_ref=near.at[d, a, :, cols],
            send_sem=e1_send.at[d, g, a], recv_sem=e1_recv.at[d, g, a],
            device_id=target[d], device_id_type=MESH_ID,
        )

    def second(d, g):
        return pltpu.make_async_remote_copy(
            src_ref=stage.at[d, :, :, columns(g * WIDE, WIDE)],
            dst_ref=near.at[d, :, :, columns(SPLIT + g * WIDE, WIDE)],
            send_sem=e2_send.at[d, g], recv_sem=e2_recv.at[d, g],
            device_id=target[d], device_id_type=MESH_ID,
        )

    def third(d, g):
        cols = columns(g * WIDE, WIDE)
        return pltpu.make_async_remote_copy(
            src_ref=result.at[d, :, :, cols], dst_ref=late.at[d, :, :, cols],
            send_sem=late_send.at[d, g], recv_sem=late_recv.at[d, g],
            device_id=target[d], device_id_type=MESH_ID,
        )

    def out_copy(a, half, g):
        cols = columns(half * SPLIT + g * WIDE, WIDE)
        return pltpu.make_async_copy(done.at[a, :, cols], outputs[a].at[:, cols], out_sem.at[half, g, a])

    for a in range(4):
        own_copy(a).start()
    barrier = pltpu.get_barrier_semaphore()
    for d in range(2):
        pl.semaphore_signal(barrier, inc=1, device_id=target[d], device_id_type=MESH_ID)
    pl.semaphore_wait(barrier, 2)
    for g in range(GROUPS):
        for d in range(2):
            for a in range(4):
                first(d, g, a).start()

    tiles = [lax.rem(me + n + t, n) for t in range(-2, 3)]
    rows = [ids_ref[pl.ds(t, 1), :].astype(jnp.float32) for t in tiles]
    eye = lax.broadcasted_iota(jnp.int32, (TILE, TILE), 0) == lax.broadcasted_iota(jnp.int32, (TILE, TILE), 1)

    def upright(row):
        return jnp.sum(jnp.where(eye, jnp.broadcast_to(row, (TILE, TILE)), 0.0), axis=1, keepdims=True)

    def middle(t):
        before = rows[t - 1][:, TILE - 1 :]
        head, tail = rows[t][:, :1], rows[t][:, TILE - 1 :]
        after = rows[t + 1][:, :1]
        return (before == head) & (head == tail) & (tail == after)

    mid_left, mid_own, mid_right = middle(1), middle(2), middle(3)
    pair_codes = pairs_ref[:, 0:1] * n + pairs_ref[:, 1:2]

    def is_listed(x, y):
        hit = (pair_codes == tiles[x] * n + tiles[y]) | (pair_codes == tiles[y] * n + tiles[x])
        return jnp.max(jnp.where(hit, 1.0, 0.0), axis=0, keepdims=True) > 0.5

    ids_a = [
        jnp.where(mid_left, rows[0], -1.0), rows[1], rows[2], rows[3], jnp.where(mid_right, rows[4], -2.0),
    ]
    ids_b = [jnp.where(mid_left, -1.0, rows[1]), rows[2], jnp.where(mid_right, -2.0, rows[3])]
    up_a = [upright(r) for r in ids_a]
    up_b = [upright(r) for r in ids_b]
    flags = {}
    for x in range(5):
        for y in range(x, min(x + 3, 5)):
            flags[x, y] = is_listed(x, y)
            flags[y, x] = flags[x, y]
    for x in range(5):
        for y in range(5):
            if (x, y) in flags:
                seen = (up_a[x] == ids_a[y]) & flags[x, y]
                bias_a[x * TILE : (x + 1) * TILE, y * TILE : (y + 1) * TILE] = jnp.where(seen, 0.0, FAR)
    for x in range(3):
        for y in range(3):
            seen = (up_b[x] == ids_b[y]) & flags[x + 1, y + 1]
            bias_b[x * TILE : (x + 1) * TILE, y * TILE : (y + 1) * TILE] = jnp.where(seen, 0.0, FAR)
    own_up = upright(rows[2])
    from_left = (own_up == rows[1][:, TILE - 1 :]) & mid_left
    from_right = (own_up == rows[3][:, :1]) & mid_right

    for a in range(4):
        own_copy(a).wait()

    def pass_on(g, carry):
        src = columns(g * WIDE, WIDE)
        for d in range(2):
            for a in range(4):
                first(d, g, a).wait_recv()
            for a in range(4):
                stage[d, a, :, src] = jnp.where(
                    mid_own, near[d, a, :, src], own[a, :, columns(SPLIT + g * WIDE, WIDE)]
                )
            second(d, g).start()
        return carry

    lax.fori_loop(0, GROUPS, pass_on, 0)

    def softmax_parts(query, grads, keys, values, bias):
        scores = dot_nt(query, keys) * (SCALE * LOG2E) + bias
        top = jnp.max(scores, axis=1, keepdims=True)
        weights = jnp.exp2(scores - top)
        inverse = 1.0 / jnp.sum(weights, axis=1, keepdims=True)
        dprobs = dot_nt(grads, values)
        delta = jnp.sum(weights * dprobs, axis=1, keepdims=True) * inverse
        return weights, inverse, dprobs, delta

    def second_half(col):
        at = columns(SPLIT + col, HEAD)
        q, k, v, g = [
            jnp.concatenate([near[0, a, :, at], own[a, :, at], near[1, a, :, at]], axis=0) for a in range(4)
        ]
        probs, dscores = [], []
        where = ((result, 1), (done, None), (result, 0))

        def put(x, a, value):
            ref, d = where[x]
            if d is None:
                ref[a, :, at] = value.astype(jnp.bfloat16)
            else:
                ref[d, a, :, columns(col, HEAD)] = value.astype(jnp.bfloat16)

        for x in range(3):
            r = slice(x * TILE, (x + 1) * TILE)
            weights, inverse, dprobs, delta = softmax_parts(q[r], g[r], k, v, bias_b[r, :])
            p = weights * inverse
            p_low = p.astype(jnp.bfloat16)
            ds = (p * (dprobs - delta)).astype(jnp.bfloat16)
            put(x, 0, dot_nn(p_low, v))
            put(x, 1, dot_nn(ds, k) * SCALE)
            probs.append(p_low)
            dscores.append(ds)
        grad_k = dot_tn(jnp.concatenate(dscores, axis=0), q) * SCALE
        grad_v = dot_tn(jnp.concatenate(probs, axis=0), g)
        for x in range(3):
            r = slice(x * TILE, (x + 1) * TILE)
            put(x, 2, grad_k[r])
            put(x, 3, grad_v[r])

    def first_half(col):
        at, far = columns(col, HEAD), columns(SPLIT + col, HEAD)
        q, k, v, g = [
            jnp.concatenate(
                [near[0, a, :, far], near[0, a, :, at], own[a, :, at], near[1, a, :, at], near[1, a, :, far]], axis=0
            )
            for a in range(4)
        ]
        probs, dscores = [], []
        for x in range(5):
            lo, hi = max(x - 2, 0) * TILE, min(x + 3, 5) * TILE
            if x == 1:
                hi = 4 * TILE
            if x == 3:
                lo = TILE
            r = slice(x * TILE, (x + 1) * TILE)
            weights, inverse, dprobs, delta = softmax_parts(q[r], g[r], k[lo:hi], v[lo:hi], bias_a[r, lo:hi])
            if x == 2:
                p = weights * inverse
                p_low = p.astype(jnp.bfloat16)
                ds = (p * (dprobs - delta)).astype(jnp.bfloat16)
                done[0, :, at] = dot_nn(p_low, v).astype(jnp.bfloat16)
                done[1, :, at] = (dot_nn(ds, k) * SCALE).astype(jnp.bfloat16)
                probs.append(p_low[:, 2 * TILE : 3 * TILE])
                dscores.append(ds[:, 2 * TILE : 3 * TILE])
            else:
                mine = slice(2 * TILE - lo, 3 * TILE - lo)
                p = weights[:, mine] * inverse
                probs.append(p.astype(jnp.bfloat16))
                dscores.append((p * (dprobs[:, mine] - delta)).astype(jnp.bfloat16))
        done[2, :, at] = (dot_tn(jnp.concatenate(dscores, axis=0), q) * SCALE).astype(jnp.bfloat16)
        done[3, :, at] = dot_tn(jnp.concatenate(probs, axis=0), g).astype(jnp.bfloat16)

    def work(g, carry):
        for d in range(2):
            second(d, g).wait_recv()
        def heads_b(j, c):
            second_half(g * WIDE + j * HEAD)
            return c

        def heads_a(j, c):
            first_half(g * WIDE + j * HEAD)
            return c

        lax.fori_loop(0, PER, heads_b, 0)
        for d in range(2):
            third(d, g).start()
        lax.fori_loop(0, PER, heads_a, 0)
        for a in range(4):
            out_copy(a, 0, g).start()
        return carry

    lax.fori_loop(0, GROUPS, work, 0)

    def finish(g, carry):
        cols = columns(g * WIDE, WIDE)
        at = columns(SPLIT + g * WIDE, WIDE)
        for d in range(2):
            third(d, g).wait_recv()
        for a in range(4):
            mixed = jnp.where(from_left, late[0, a, :, cols], done[a, :, at])
            done[a, :, at] = jnp.where(from_right, late[1, a, :, cols], mixed)
        for a in range(4):
            out_copy(a, 1, g).start()
        return carry

    lax.fori_loop(0, GROUPS, finish, 0)

    def drain(g, carry):
        for d in range(2):
            for a in range(4):
                first(d, g, a).wait_send()
            second(d, g).wait_send()
            third(d, g).wait_send()
        for half in range(2):
            for a in range(4):
                out_copy(a, half, g).wait()
        return carry

    lax.fori_loop(0, GROUPS, drain, 0)


def solution(mesh):
    n_dp, n_ctx = mesh.shape["dp"], mesh.shape["ctx"]
    token_spec = P(("dp", "ctx"), None)

    def body(queries, keys, values, grad_out, doc_ids, tile_pairs):
        shape = jax.ShapeDtypeStruct(queries.shape, jnp.bfloat16)
        width = queries.shape[1]
        any_space = pl.BlockSpec(memory_space=pl.ANY)
        in_vmem = pl.BlockSpec(memory_space=pltpu.VMEM)
        low = jnp.bfloat16
        sem = pltpu.SemaphoreType.DMA
        return pl.pallas_call(
            functools.partial(kernel, n_dp, n_ctx),
            out_shape=(shape,) * 4,
            in_specs=[any_space] * 4 + [in_vmem] * 2,
            out_specs=(any_space,) * 4,
            scratch_shapes=[
                pltpu.VMEM((4, TILE, width), low),
                pltpu.VMEM((2, 4, TILE, width), low),
                pltpu.VMEM((2, 4, TILE, SPLIT), low),
                pltpu.VMEM((2, 4, TILE, SPLIT), low),
                pltpu.VMEM((2, 4, TILE, SPLIT), low),
                pltpu.VMEM((4, TILE, width), low),
                pltpu.VMEM((5 * TILE, 5 * TILE), jnp.float32),
                pltpu.VMEM((3 * TILE, 3 * TILE), jnp.float32),
                sem((4,)),
                sem((2, GROUPS, 4)),
                sem((2, GROUPS, 4)),
                sem((2, GROUPS)),
                sem((2, GROUPS)),
                sem((2, GROUPS)),
                sem((2, GROUPS)),
                sem((2, GROUPS, 4)),
            ],
            compiler_params=pltpu.CompilerParams(
                collective_id=0, has_side_effects=True, vmem_limit_bytes=48 * 1024 * 1024
            ),
        )(queries, keys, values, grad_out, doc_ids.reshape(-1, TILE), tile_pairs)

    return jax.shard_map(
        body,
        mesh=mesh,
        in_specs=(token_spec,) * 4 + (P(), P()),
        out_specs=(token_spec,) * 4,
        check_vma=False,
    )
```

```python
import functools
import math

import jax
import jax.numpy as jnp
from jax import lax
from jax.experimental import pallas as pl
from jax.experimental.pallas import tpu as pltpu
from jax.sharding import PartitionSpec as P

HEAD = 128
TILE = 128
HEADS = 16
HALF = 8
PER = 2
GROUPS = HALF // PER
WIDE = PER * HEAD
BLOCKS = 4
MOST = 12
GRAIN = 16
GRAINS = TILE // GRAIN
PLANS = (8, 10, 11, 12)
PIECE = {8: 8, 10: 4, 11: 3, 12: 2}
SCALE = 1.0 / math.sqrt(HEAD)
LOG2E = math.log2(math.e)
FAR = -1e30
MESH_ID = pl.DeviceIdType.MESH


def dot_nt(a, b):
    return lax.dot_general(a, b, (((1,), (1,)), ((), ())), preferred_element_type=jnp.float32)


def dot_nn(a, b):
    return lax.dot_general(a, b, (((1,), (0,)), ((), ())), preferred_element_type=jnp.float32)


def dot_tn(a, b):
    return lax.dot_general(a, b, (((0,), (0,)), ((), ())), preferred_element_type=jnp.float32)


def columns(start, size):
    return pl.ds(pl.multiple_of(start, HEAD), size)


def head_cols(h):
    return slice(h * HEAD, (h + 1) * HEAD)


def grain_rows(start, count):
    return slice(start * GRAIN, (start + count) * GRAIN)


def piece_grain(d, plan, t):
    return GRAINS - PIECE[plan] + t if d == 0 else t


def piece_place(plan, h, t):
    place = h * PIECE[plan] + t
    first = 8 if plan == 8 else plan
    return first + place // GRAINS, place % GRAINS


def relay_source(d, plan, slot, grain):
    first = 8 if plan == 8 else plan
    if slot < first:
        return None
    place = (slot - first) * GRAINS + grain
    h, t = place // PIECE[plan], place % PIECE[plan]
    return (h, piece_grain(d, plan, t)) if h < plan else None


def relay_target(d, plan, h, grain):
    if h >= plan:
        return None
    t = grain - piece_grain(d, plan, 0)
    return piece_place(plan, h, t) if 0 <= t < PIECE[plan] else None


def result_place(plan, h, grain):
    if h >= 12:
        return (h - 12, grain)
    if plan == 8 and grain < 4:
        return (h - 8, grain + 4)
    if plan == 10 and h >= 10 and grain < 5:
        return (2 * (h - 10) + grain // 3, 5 + grain % 3)
    if plan == 11 and h == 11 and grain < 6:
        return (grain // 2, 6 + grain % 2)
    return None


def result_source(plan, block, grain):
    for h in range(8, 12):
        for g in range(GRAINS):
            if result_place(plan, h, g) == (block, grain):
                return (h, g)
    return None


def mirrored(d, grain):
    return grain if d == 0 else GRAINS - 1 - grain


def mirrored_pair(d, pair):
    return None if pair is None else (pair[0], mirrored(d, pair[1]))


def runs(entries):
    start = 0
    for at in range(1, GRAINS + 1):
        joined = at < GRAINS and all(
            (a is None and b is None) or (a is not None and b is not None and a[0] == b[0] and b[1] == a[1] + 1)
            for a, b in zip(entries[at - 1], entries[at])
        )
        if not joined:
            yield start, at - start, entries[start]
            start = at


def kernel(
    n_dp, n_ctx,
    q_ref, k_ref, v_ref, g_ref, ids_hbm, pairs_hbm,
    done,
    own, near, stage, far, result, pack, late, bias, ids_ref, pairs_ref,
    own_sem, side_sem, e1_send, e1_recv, e2_send, e2_recv, late_send, late_recv,
):
    n = n_dp * n_ctx
    me = lax.axis_index("dp") * n_ctx + lax.axis_index("ctx")
    right = lax.rem(me + 1, n)
    left = lax.rem(me + n - 1, n)
    target = [(x // n_ctx, lax.rem(x, n_ctx)) for x in (right, left)]
    inputs = (q_ref, k_ref, v_ref, g_ref)

    def own_copy(a):
        return pltpu.make_async_copy(inputs[a], own.at[a], own_sem.at[a])

    side_copies = [
        pltpu.make_async_copy(ids_hbm, ids_ref, side_sem.at[0]),
        pltpu.make_async_copy(pairs_hbm, pairs_ref, side_sem.at[1]),
    ]

    def first(d, g):
        cols = columns(g * WIDE, WIDE)
        return pltpu.make_async_remote_copy(
            src_ref=own.at[:, :, cols], dst_ref=near.at[d, :, :, cols],
            send_sem=e1_send.at[d, g], recv_sem=e1_recv.at[d, g],
            device_id=target[d], device_id_type=MESH_ID,
        )

    def second(d, s):
        return pltpu.make_async_remote_copy(
            src_ref=stage.at[d, :, :, columns(s * HEAD, HEAD)],
            dst_ref=near.at[d, :, :, columns((HALF + s) * HEAD, HEAD)],
            send_sem=e2_send.at[d, s], recv_sem=e2_recv.at[d, s],
            device_id=target[d], device_id_type=MESH_ID,
        )

    def third(d, j):
        cols = columns(j * HEAD, HEAD)
        return pltpu.make_async_remote_copy(
            src_ref=pack.at[d, :, :, cols], dst_ref=late.at[d, :, :, cols],
            send_sem=late_send.at[d, j], recv_sem=late_recv.at[d, j],
            device_id=target[d], device_id_type=MESH_ID,
        )

    barrier = pltpu.get_barrier_semaphore()
    for d in range(2):
        pl.semaphore_signal(barrier, inc=1, device_id=target[d], device_id_type=MESH_ID)
    for copy in side_copies:
        copy.start()
    for a in range(4):
        own_copy(a).start()
    pl.semaphore_wait(barrier, 2)
    for a in range(4):
        own_copy(a).wait()
    for g in range(GROUPS):
        for d in range(2):
            first(d, g).start()

    for copy in side_copies:
        copy.wait()
    tiles = [lax.rem(me + n + t, n) for t in range(-2, 3)]
    rows = [ids_ref[pl.ds(t, 1), :].astype(jnp.float32) for t in tiles]
    eye = lax.broadcasted_iota(jnp.int32, (TILE, TILE), 0) == lax.broadcasted_iota(jnp.int32, (TILE, TILE), 1)

    def upright(row):
        return jnp.sum(jnp.where(eye, jnp.broadcast_to(row, (TILE, TILE)), 0.0), axis=1, keepdims=True)

    def middle(t):
        before = rows[t - 1][:, TILE - 1 :]
        head, tail = rows[t][:, :1], rows[t][:, TILE - 1 :]
        after = rows[t + 1][:, :1]
        return (before == head) & (head == tail) & (tail == after)

    def plans_of(middle_tile, far_tile):
        count = jnp.sum(jnp.where(rows[far_tile] == rows[middle_tile][:, :1], 1.0, 0.0), axis=1, keepdims=True)
        return {12: count < 33, 11: (count > 32) & (count < 49), 10: (count > 48) & (count < 65), 8: count > 64}

    mid_left, mid_own, mid_right = middle(1), middle(2), middle(3)
    send_plan = [{p: c & mid_own for p, c in plans_of(2, f).items()} for f in (1, 3)]
    recv_plan = [plans_of(1, 0), plans_of(3, 4)]
    codes = pairs_ref[0:1, :] * n + pairs_ref[1:2, :]

    def is_listed(x, y):
        hit = (codes == tiles[x] * n + tiles[y]) | (codes == tiles[y] * n + tiles[x])
        return jnp.max(jnp.where(hit, 1.0, 0.0), axis=1, keepdims=True) > 0.5

    up = [upright(r) for r in rows]
    flags = {}
    for x in range(5):
        for y in range(x, min(x + 3, 5)):
            flags[x, y] = is_listed(x, y)
            flags[y, x] = flags[x, y]
    for x, y in flags:
        seen = (up[x] == rows[y]) & flags[x, y]
        bias[x * TILE : (x + 1) * TILE, y * TILE : (y + 1) * TILE] = jnp.where(seen, 0.0, FAR)
    returned = [
        jnp.where((up[2] == rows[1][:, TILE - 1 :]) & mid_left, 1.0, 0.0),
        jnp.where((up[2] == rows[3][:, :1]) & mid_right, 1.0, 0.0),
    ]


    def pass_on(slot):
        for d in range(2):
            entries = [
                [(slot, grain)] + [relay_source(d, plan, slot, grain) for plan in PLANS] for grain in range(GRAINS)
            ]
            for start, count, sources in runs(entries):
                value = own[:, grain_rows(start, count), head_cols(slot)]
                for plan, source in zip(PLANS, sources[1:]):
                    if source is not None:
                        other = near[d, :, grain_rows(source[1], count), head_cols(source[0])]
                        value = jnp.where(send_plan[d][plan], other, value)
                stage[d, :, grain_rows(start, count), head_cols(slot - HALF)] = value
            second(d, slot - HALF).start()

    def gather_far(h):
        for d in range(2):
            entries = [
                [relay_target(d, plan, h, grain) or (None if plan != 8 else (8, grain)) for plan in PLANS]
                for grain in range(GRAINS)
            ]
            for start, count, sources in runs(entries):
                value = None
                for plan, source in zip(PLANS, sources):
                    if source is not None:
                        other = near[d, :, grain_rows(source[1], count), head_cols(source[0])]
                        value = other if value is None else jnp.where(recv_plan[d][plan], other, value)
                far[d, :, grain_rows(start, count), head_cols(h)] = value

    def softmax_parts(query, grads, keys, values, mask):
        scores = dot_nt(query, keys) * (SCALE * LOG2E) + mask
        top = jnp.max(scores, axis=1, keepdims=True)
        weights = jnp.exp2(scores - top)
        inverse = 1.0 / jnp.sum(weights, axis=1, keepdims=True)
        dprobs = dot_nt(grads, values)
        delta = jnp.sum(weights * dprobs, axis=1, keepdims=True) * inverse
        return weights, inverse, dprobs, delta

    def three_tiles(h):
        at = columns(h * HEAD, HEAD)
        back = columns((h - HALF) * HEAD, HEAD)
        q, k, v, g = [
            jnp.concatenate([near[0, a, :, at], own[a, :, at], near[1, a, :, at]], axis=0) for a in range(4)
        ]
        probs, dscores = [], []

        def put(x, a, value):
            if x == 1:
                done[a, :, at] = value.astype(jnp.bfloat16)
            else:
                result[1 if x == 0 else 0, a, :, back] = value.astype(jnp.bfloat16)

        for x in range(3):
            r = slice(x * TILE, (x + 1) * TILE)
            mask = bias[(x + 1) * TILE : (x + 2) * TILE, TILE : 4 * TILE]
            weights, inverse, dprobs, delta = softmax_parts(q[r], g[r], k, v, mask)
            p = weights * inverse
            p_low = p.astype(jnp.bfloat16)
            ds = (p * (dprobs - delta)).astype(jnp.bfloat16)
            put(x, 0, dot_nn(p_low, v))
            put(x, 1, dot_nn(ds, k) * SCALE)
            probs.append(p_low)
            dscores.append(ds)
        grad_k = dot_tn(jnp.concatenate(dscores, axis=0), q) * SCALE
        grad_v = dot_tn(jnp.concatenate(probs, axis=0), g)
        for x in range(3):
            r = slice(x * TILE, (x + 1) * TILE)
            put(x, 2, grad_k[r])
            put(x, 3, grad_v[r])

    def five_tiles(h):
        at = columns(h * HEAD, HEAD)
        q, k, v, g = [
            jnp.concatenate(
                [far[0, a, :, at], near[0, a, :, at], own[a, :, at], near[1, a, :, at], far[1, a, :, at]], axis=0
            )
            for a in range(4)
        ]
        probs, dscores = [], []
        for x, lo, hi in ((0, 0, 3), (1, 0, 4), (2, 0, 5), (3, 1, 5), (4, 2, 5)):
            r = slice(x * TILE, (x + 1) * TILE)
            c = slice(lo * TILE, hi * TILE)
            weights, inverse, dprobs, delta = softmax_parts(q[r], g[r], k[c], v[c], bias[r, c])
            mine = slice((2 - lo) * TILE, (3 - lo) * TILE)
            if x == 2:
                p = weights * inverse
                p_low = p.astype(jnp.bfloat16)
                ds = (p * (dprobs - delta)).astype(jnp.bfloat16)
                done[0, :, at] = dot_nn(p_low, v).astype(jnp.bfloat16)
                done[1, :, at] = (dot_nn(ds, k) * SCALE).astype(jnp.bfloat16)
                probs.append(p_low[:, mine])
                dscores.append(ds[:, mine])
            else:
                p = weights[:, mine] * inverse
                probs.append(p.astype(jnp.bfloat16))
                dscores.append((p * (dprobs[:, mine] - delta)).astype(jnp.bfloat16))
        done[2, :, at] = (dot_tn(jnp.concatenate(dscores, axis=0), q) * SCALE).astype(jnp.bfloat16)
        done[3, :, at] = dot_tn(jnp.concatenate(probs, axis=0), g).astype(jnp.bfloat16)

    def send_back(j):
        for d in range(2):
            entries = [
                [(12 + j, grain)]
                + [mirrored_pair(d, result_source(plan, j, mirrored(d, grain))) for plan in PLANS]
                for grain in range(GRAINS)
            ]
            for start, count, sources in runs(entries):
                value = result[d, :, grain_rows(start, count), head_cols(4 + j)]
                for plan, source in zip(PLANS, sources[1:]):
                    if source is not None:
                        other = result[d, :, grain_rows(source[1], count), head_cols(source[0] - HALF)]
                        value = jnp.where(send_plan[d][plan], other, value)
                pack[d, :, grain_rows(start, count), head_cols(j)] = value
            third(d, j).start()

    def take_back(h):
        for d in range(2):
            entries = [
                [mirrored_pair(d, result_place(plan, h, mirrored(d, grain))) for plan in PLANS]
                for grain in range(GRAINS)
            ]
            for start, count, sources in runs(entries):
                r = grain_rows(start, count)
                for plan, source in zip(PLANS, sources):
                    if source is None or (h >= 12 and plan != 8):
                        continue
                    take = returned[d][r] > 0.5
                    if h < 12:
                        take = take & recv_plan[d][plan]
                    for a in range(4):
                        other = late[d, a, grain_rows(source[1], count), head_cols(source[0])]
                        done[a, r, head_cols(h)] = jnp.where(take, other, done[a, r, head_cols(h)])

    early_slots = ((8, 9), (10, 11), (12,), (13,))
    for g in range(GROUPS):
        for d in range(2):
            first(d, g).wait_recv()
        for slot in early_slots[g]:
            pass_on(slot)

    ready = ((0, 1, 2, 3), (4, 5), (6, 8, 9, 11), (7, 10))

    def work(h, carry):
        for d in range(2):
            second(d, h - HALF).wait_recv()

        @pl.when(h == 11)
        def _():
            pass_on(14)
            pass_on(15)

        three_tiles(h)
        for j in range(BLOCKS):

            @pl.when(h == 12 + j)
            def _():
                send_back(j)
                for other in ready[j]:
                    gather_far(other)

        @pl.when(h >= 12)
        def _():
            lax.fori_loop(0, 2, lambda i, c: (five_tiles(2 * (h - 12) + i), c)[1], 0)

        return carry

    lax.fori_loop(HALF, HEADS, work, 0)
    lax.fori_loop(HALF, MOST, lambda h, c: (five_tiles(h), c)[1], 0)

    for j in range(BLOCKS):
        for d in range(2):
            third(d, j).wait_recv()
        take_back(12 + j)
        take_back(8 + j)

    for d in range(2):
        for g in range(GROUPS):
            first(d, g).wait_send()
        for s in range(HALF):
            second(d, s).wait_send()
        for j in range(BLOCKS):
            third(d, j).wait_send()


def write_out(done, att_ref, gq_ref, gk_ref, gv_ref, out_sem):
    copies = [
        pltpu.make_async_copy(done.at[a], ref, out_sem.at[a])
        for a, ref in enumerate((att_ref, gq_ref, gk_ref, gv_ref))
    ]
    for copy in copies:
        copy.start()
    for copy in copies:
        copy.wait()


def solution(mesh):
    n_dp, n_ctx = mesh.shape["dp"], mesh.shape["ctx"]
    token_spec = P(("dp", "ctx"), None)

    def body(queries, keys, values, grad_out, doc_ids, tile_pairs):
        width = queries.shape[1]
        in_hbm = pl.BlockSpec(memory_space=pltpu.HBM)
        low = jnp.bfloat16
        sem = pltpu.SemaphoreType.DMA
        held = [
            pltpu.with_memory_space_constraint(x, pltpu.HBM)
            for x in (queries, keys, values, grad_out, doc_ids.reshape(-1, TILE), tile_pairs.T)
        ]
        done = pl.pallas_call(
            functools.partial(kernel, n_dp, n_ctx),
            out_shape=jax.ShapeDtypeStruct((4, TILE, width), low),
            in_specs=[in_hbm] * 6,
            out_specs=pl.BlockSpec(memory_space=pltpu.VMEM),
            scratch_shapes=[
                pltpu.VMEM((4, TILE, width), low),
                pltpu.VMEM((2, 4, TILE, width), low),
                pltpu.VMEM((2, 4, TILE, HALF * HEAD), low),
                pltpu.VMEM((2, 4, TILE, MOST * HEAD), low),
                pltpu.VMEM((2, 4, TILE, HALF * HEAD), low),
                pltpu.VMEM((2, 4, TILE, BLOCKS * HEAD), low),
                pltpu.VMEM((2, 4, TILE, BLOCKS * HEAD), low),
                pltpu.VMEM((5 * TILE, 5 * TILE), jnp.float32),
                pltpu.VMEM((doc_ids.shape[0] // TILE, TILE), jnp.int32),
                pltpu.VMEM((2, tile_pairs.shape[0]), jnp.int32),
                sem((4,)),
                sem((2,)),
                sem((2, GROUPS)),
                sem((2, GROUPS)),
                sem((2, HALF)),
                sem((2, HALF)),
                sem((2, BLOCKS)),
                sem((2, BLOCKS)),
            ],
            compiler_params=pltpu.CompilerParams(
                collective_id=0, has_side_effects=True, vmem_limit_bytes=48 * 1024 * 1024
            ),
        )(*held)
        shape = jax.ShapeDtypeStruct(queries.shape, low)
        return pl.pallas_call(
            write_out,
            out_shape=(shape,) * 4,
            in_specs=[pl.BlockSpec(memory_space=pl.ANY)],
            out_specs=(in_hbm,) * 4,
            scratch_shapes=[sem((4,))],
            compiler_params=pltpu.CompilerParams(vmem_limit_bytes=1024 * 1024),
        )(done)

    return jax.shard_map(
        body,
        mesh=mesh,
        in_specs=(token_spec,) * 4 + (P(), P()),
        out_specs=(token_spec,) * 4,
        check_vma=False,
    )
```

```python
import functools
import math

import jax
import jax.numpy as jnp
from jax import lax
from jax.experimental import pallas as pl
from jax.experimental.pallas import tpu as pltpu
from jax.sharding import PartitionSpec as P

HEAD = 128
TILE = 128
HEADS = 16
HALF = 8
PER = 2
GROUPS = HALF // PER
WIDE = PER * HEAD
BLOCKS = 4
MOST = 12
GRAIN = 16
GRAINS = TILE // GRAIN
PLANS = (8, 10, 11, 12)
PIECE = {8: 8, 10: 4, 11: 3, 12: 2}
ORDER = {8: (12, 11, 10, 9, 8, 13, 14, 15), 10: (12, 11, 10, 13, 14), 11: (12, 11, 13, 14, 15), 12: (12, 13, 14)}
SCALE = 1.0 / math.sqrt(HEAD)
LOG2E = math.log2(math.e)
FAR = -1e30
MESH_ID = pl.DeviceIdType.MESH


def dot_nt(a, b):
    return lax.dot_general(a, b, (((1,), (1,)), ((), ())), preferred_element_type=jnp.float32)


def dot_nn(a, b):
    return lax.dot_general(a, b, (((1,), (0,)), ((), ())), preferred_element_type=jnp.float32)


def dot_tn(a, b):
    return lax.dot_general(a, b, (((0,), (0,)), ((), ())), preferred_element_type=jnp.float32)


def columns(start, size):
    return pl.ds(pl.multiple_of(start, HEAD), size)


def head_cols(h):
    return slice(h * HEAD, (h + 1) * HEAD)


def grain_rows(start, count):
    return slice(start * GRAIN, (start + count) * GRAIN)


def piece_grain(d, plan, t):
    return GRAINS - PIECE[plan] + t if d == 0 else t


def piece_place(plan, h, t):
    place = h * PIECE[plan] + t
    return ORDER[plan][place // GRAINS], place % GRAINS


def relay_source(d, plan, slot, grain):
    if slot not in ORDER[plan]:
        return None
    place = ORDER[plan].index(slot) * GRAINS + grain
    h, t = place // PIECE[plan], place % PIECE[plan]
    return (h, piece_grain(d, plan, t)) if h < plan else None


def relay_target(d, plan, h, grain):
    if h >= plan:
        return None
    t = grain - piece_grain(d, plan, 0)
    return piece_place(plan, h, t) if 0 <= t < PIECE[plan] else None


def result_place(plan, h, grain):
    if h >= 12:
        return (h - 12, grain)
    if plan == 8 and grain < 4:
        return (h - 8, grain + 4)
    if plan == 10 and h >= 10 and grain < 5:
        return (2 * (h - 10) + grain // 3, 5 + grain % 3)
    if plan == 11 and h == 11 and grain < 6:
        return (grain // 2, 6 + grain % 2)
    return None


def result_source(plan, block, grain):
    for h in range(8, 12):
        for g in range(GRAINS):
            if result_place(plan, h, g) == (block, grain):
                return (h, g)
    return None


def mirrored(d, grain):
    return grain if d == 0 else GRAINS - 1 - grain


def mirrored_pair(d, pair):
    return None if pair is None else (pair[0], mirrored(d, pair[1]))


def runs(entries):
    start = 0
    for at in range(1, GRAINS + 1):
        joined = at < GRAINS and all(
            (a is None and b is None) or (a is not None and b is not None and a[0] == b[0] and b[1] == a[1] + 1)
            for a, b in zip(entries[at - 1], entries[at])
        )
        if not joined:
            yield start, at - start, entries[start]
            start = at


def kernel(
    n_dp, n_ctx,
    q_ref, k_ref, v_ref, g_ref, ids_hbm, pairs_hbm,
    done,
    own, near, stage, far, result, pack, late, mask_wide, mask_left, mask_right, from_right, row_kind, ids_ref, pairs_ref,
    own_sem, side_sem, e1_send, e1_recv, e2_send, e2_recv, late_send, late_recv,
):
    n = n_dp * n_ctx
    me = lax.axis_index("dp") * n_ctx + lax.axis_index("ctx")
    right = lax.rem(me + 1, n)
    left = lax.rem(me + n - 1, n)
    target = [(x // n_ctx, lax.rem(x, n_ctx)) for x in (right, left)]
    inputs = (q_ref, k_ref, v_ref, g_ref)

    def own_copy(a):
        return pltpu.make_async_copy(inputs[a], own.at[a], own_sem.at[a])

    side_copies = [
        pltpu.make_async_copy(ids_hbm, ids_ref, side_sem.at[0]),
        pltpu.make_async_copy(pairs_hbm, pairs_ref, side_sem.at[1]),
    ]

    def first(d, g):
        cols = columns(g * WIDE, WIDE)
        return pltpu.make_async_remote_copy(
            src_ref=own.at[:, :, cols], dst_ref=near.at[d, :, :, cols],
            send_sem=e1_send.at[d, g], recv_sem=e1_recv.at[d, g],
            device_id=target[d], device_id_type=MESH_ID,
        )

    def second(d, s):
        return pltpu.make_async_remote_copy(
            src_ref=stage.at[d, :, :, columns(s * HEAD, HEAD)],
            dst_ref=near.at[d, :, :, columns((HALF + s) * HEAD, HEAD)],
            send_sem=e2_send.at[d, s], recv_sem=e2_recv.at[d, s],
            device_id=target[d], device_id_type=MESH_ID,
        )

    def third(d, j):
        cols = columns(j * HEAD, HEAD)
        return pltpu.make_async_remote_copy(
            src_ref=pack.at[d, :, :, cols], dst_ref=late.at[d, :, :, cols],
            send_sem=late_send.at[d, j], recv_sem=late_recv.at[d, j],
            device_id=target[d], device_id_type=MESH_ID,
        )

    barrier = pltpu.get_barrier_semaphore()
    for d in range(2):
        pl.semaphore_signal(barrier, inc=1, device_id=target[d], device_id_type=MESH_ID)
    for copy in side_copies:
        copy.start()
    for a in range(4):
        own_copy(a).start()
    pl.semaphore_wait(barrier, 2)
    for a in range(4):
        own_copy(a).wait()
    for g in range(GROUPS):
        for d in range(2):
            first(d, g).start()

    for copy in side_copies:
        copy.wait()
    tiles = [lax.rem(me + n + t, n) for t in range(-2, 3)]
    rows = [ids_ref[pl.ds(t, 1), :].astype(jnp.float32) for t in tiles]
    eye = lax.broadcasted_iota(jnp.int32, (TILE, TILE), 0) == lax.broadcasted_iota(jnp.int32, (TILE, TILE), 1)

    def upright(row):
        return jnp.sum(jnp.where(eye, jnp.broadcast_to(row, (TILE, TILE)), 0.0), axis=1, keepdims=True)

    def middle(t):
        before = rows[t - 1][:, TILE - 1 :]
        head, tail = rows[t][:, :1], rows[t][:, TILE - 1 :]
        after = rows[t + 1][:, :1]
        return (before == head) & (head == tail) & (tail == after)

    def plans_of(middle_tile, far_tile):
        count = jnp.sum(jnp.where(rows[far_tile] == rows[middle_tile][:, :1], 1.0, 0.0), axis=1, keepdims=True)
        return {12: count < 33, 11: (count > 32) & (count < 49), 10: (count > 48) & (count < 65), 8: count > 64}

    mid_left, mid_own, mid_right = middle(1), middle(2), middle(3)
    send_plan = [{p: c & mid_own for p, c in plans_of(2, f).items()} for f in (1, 3)]
    recv_plan = [plans_of(1, 0), plans_of(3, 4)]
    codes = pairs_ref[0:1, :] * n + pairs_ref[1:2, :]

    def is_listed(x, y):
        hit = (codes == tiles[x] * n + tiles[y]) | (codes == tiles[y] * n + tiles[x])
        return jnp.max(jnp.where(hit, 1.0, 0.0), axis=1, keepdims=True)

    up = [upright(r) for r in rows]
    flags = {}
    for x in range(5):
        for y in range(x, min(x + 3, 5)):
            flags[x, y] = is_listed(x, y)
            flags[y, x] = flags[x, y]

    def number(condition):
        return jnp.where(condition, 1.0, 0.0)

    def plain(x):
        return rows[x], up[x], [(x, None, None)]

    def mixed(x, y, along, across):
        return (
            jnp.where(along > 0.5, rows[x], rows[y]),
            jnp.where(across > 0.5, up[x], up[y]),
            [(x, along, across), (y, 1.0 - along, 1.0 - across)],
        )

    def mask_of(query_tile, key_tile, keep=None):
        listed = jnp.zeros((TILE, TILE), jnp.float32)
        for x, _, across in query_tile[2]:
            for y, along, _ in key_tile[2]:
                if (x, y) in flags:
                    share = jnp.broadcast_to(flags[x, y], (TILE, TILE))
                    share = share if across is None else share * across
                    listed += share if along is None else share * along
        if keep is not None:
            listed = listed * keep
        return jnp.where((query_tile[1] == key_tile[0]) & (listed > 0.5), 0.0, FAR)

    far_left = [number((r[0] == rows[1][:, :1]) & mid_left) for r in (rows, up)]
    far_right = [number((r[4] == rows[3][:, :1]) & mid_right) for r in (rows, up)]
    take_right = [number((r[1] != rows[2][:, :1]) & mid_own) for r in (rows, up)]
    far_rows = (far_left[1], far_right[1])
    centre = plain(2)
    after = plain(3)
    near_side = mixed(3, 1, *take_right)
    left_side = mixed(0, 2, *far_left)
    right_side = mixed(4, 2, *far_right)
    one, two, three = slice(0, TILE), slice(TILE, 2 * TILE), slice(2 * TILE, 3 * TILE)
    not_middle = 1.0 - number(mid_own)
    mask_wide[one, one] = mask_of(near_side, near_side)
    mask_wide[one, two] = mask_of(near_side, centre)
    mask_wide[two, one] = mask_of(centre, near_side)
    mask_wide[two, two] = mask_of(centre, centre)
    mask_wide[two, three] = mask_of(centre, after, not_middle)
    mask_wide[three, two] = mask_of(after, centre, not_middle)
    mask_wide[three, three] = mask_of(after, after)
    for ref, x, y in ((mask_left, left_side, near_side), (mask_right, right_side, after)):
        ref[one, one] = mask_of(x, x)
        ref[one, two] = mask_of(x, y)
        ref[two, one] = mask_of(y, x)
        ref[two, two] = mask_of(y, y)
    square = (TILE, TILE)
    from_right[...] = jnp.broadcast_to(take_right[1], square).astype(jnp.bfloat16)
    reaches_left = number(up[2] == rows[1][:, TILE - 1 :])
    reaches_right = number(up[2] == rows[3][:, :1])
    row_kind[0] = jnp.broadcast_to(reaches_left, square)
    row_kind[1] = jnp.broadcast_to(reaches_right, square)
    returned = [reaches_left * number(mid_left), reaches_right * number(mid_right)]

    def pass_on(slot):
        for d in range(2):
            entries = [
                [(slot, grain)] + [relay_source(d, plan, slot, grain) for plan in PLANS] for grain in range(GRAINS)
            ]
            for start, count, sources in runs(entries):
                value = own[:, grain_rows(start, count), head_cols(slot)]
                for plan, source in zip(PLANS, sources[1:]):
                    if source is not None:
                        other = near[d, :, grain_rows(source[1], count), head_cols(source[0])]
                        value = jnp.where(send_plan[d][plan], other, value)
                stage[d, :, grain_rows(start, count), head_cols(slot - HALF)] = value
            second(d, slot - HALF).start()

    def gather_far(h):
        for d in range(2):
            entries = [
                [relay_target(d, plan, h, grain) or (None if plan != 8 else (8, grain)) for plan in PLANS]
                for grain in range(GRAINS)
            ]
            for start, count, sources in runs(entries):
                value = None
                for plan, source in zip(PLANS, sources):
                    if source is not None:
                        other = near[d, :, grain_rows(source[1], count), head_cols(source[0])]
                        value = other if value is None else jnp.where(recv_plan[d][plan], other, value)
                r = grain_rows(start, count)
                for a in range(4):
                    far[d, a, r, head_cols(h)] = jnp.where(far_rows[d][r] > 0.5, value[a], own[a, r, head_cols(h)])

    def softmax_parts(query, grads, keys, values, mask):
        scores = dot_nt(query, keys) * (SCALE * LOG2E) + mask
        top = jnp.max(scores, axis=1, keepdims=True)
        weights = jnp.exp2(scores - top)
        inverse = 1.0 / jnp.sum(weights, axis=1, keepdims=True)
        dprobs = dot_nt(grads, values)
        delta = jnp.sum(weights * dprobs, axis=1, keepdims=True) * inverse
        return weights, inverse, dprobs, delta

    def load(h):
        at = columns(h * HEAD, HEAD)
        after_rows = [near[1, a, :, at] for a in range(4)]
        use_right = from_right[...] > 0.5
        near_rows = [jnp.where(use_right, after_rows[a], near[0, a, :, at]) for a in range(4)]
        return at, near_rows, [own[a, :, at] for a in range(4)], after_rows

    def stacked(*parts):
        return [jnp.concatenate(part, axis=0) for part in zip(*parts)]

    def full(parts):
        weights, inverse, dprobs, delta = parts
        p = weights * inverse
        return p.astype(jnp.bfloat16), (p * (dprobs - delta)).astype(jnp.bfloat16)

    def partial(parts, cols):
        weights, inverse, dprobs, delta = parts
        p = weights[:, cols] * inverse
        return p.astype(jnp.bfloat16), (p * (dprobs[:, cols] - delta)).astype(jnp.bfloat16)

    def three_tiles(h):
        at, near_rows, own_rows, after_rows = load(h)
        back = columns((h - HALF) * HEAD, HEAD)
        q, k, v, g = stacked(near_rows, own_rows, after_rows)
        wide = slice(0, 2 * TILE)
        p_near, ds_near = full(softmax_parts(q[one], g[one], k[wide], v[wide], mask_wide[one, wide]))
        p_own, ds_own = full(softmax_parts(q[two], g[two], k, v, mask_wide[two, :]))
        tail = slice(TILE, 3 * TILE)
        p_after, ds_after = partial(softmax_parts(q[three], g[three], k[tail], v[tail], mask_wide[three, tail]), one)
        result[0, :, back] = dot_nn(p_near, v[wide]).astype(jnp.bfloat16)
        result[1, :, back] = (dot_nn(ds_near, k[wide]) * SCALE).astype(jnp.bfloat16)
        result[2, :, back] = (
            dot_tn(jnp.concatenate([ds_near[:, one], ds_own[:, one]], axis=0), q[wide]) * SCALE
        ).astype(jnp.bfloat16)
        result[3, :, back] = dot_tn(
            jnp.concatenate([p_near[:, one], p_own[:, one]], axis=0), g[wide]
        ).astype(jnp.bfloat16)
        done[0, :, at] = dot_nn(p_own, v).astype(jnp.bfloat16)
        done[1, :, at] = (dot_nn(ds_own, k) * SCALE).astype(jnp.bfloat16)
        done[2, :, at] = (
            dot_tn(jnp.concatenate([ds_near[:, two], ds_own[:, two], ds_after], axis=0), q) * SCALE
        ).astype(jnp.bfloat16)
        done[3, :, at] = dot_tn(
            jnp.concatenate([p_near[:, two], p_own[:, two], p_after], axis=0), g
        ).astype(jnp.bfloat16)

    def two_tiles(first_rows, second_rows, mask):
        q, k, v, g = stacked(first_rows, second_rows)
        p_one, ds_one = full(softmax_parts(q[one], g[one], k, v, mask[one, :]))
        p_two, ds_two = partial(softmax_parts(q[two], g[two], k, v, mask[two, :]), one)
        return (
            dot_nn(p_one, v),
            dot_nn(ds_one, k) * SCALE,
            dot_tn(jnp.concatenate([ds_one[:, one], ds_two], axis=0), q) * SCALE,
            dot_tn(jnp.concatenate([p_one[:, one], p_two], axis=0), g),
        )

    def five_tiles(h):
        at, near_rows, own_rows, after_rows = load(h)
        far_sides = [[far[d, a, :, at] for a in range(4)] for d in range(2)]
        before = two_tiles(far_sides[0], near_rows, mask_left)
        behind = two_tiles(far_sides[1], after_rows, mask_right)
        q, k, v, g = own_rows
        p, ds = full(softmax_parts(q, g, k, v, mask_wide[two, two]))
        inside = (dot_nn(p, v), dot_nn(ds, k) * SCALE, dot_tn(ds, q) * SCALE, dot_tn(p, g))
        on_left, on_right = row_kind[0] > 0.5, row_kind[1] > 0.5
        for a in range(4):
            value = jnp.where(on_left, before[a], jnp.where(on_right, behind[a], inside[a]))
            done[a, :, at] = value.astype(jnp.bfloat16)

    def send_back(j):
        for d in range(2):
            entries = [
                [(12 + j, grain)]
                + [mirrored_pair(d, result_source(plan, j, mirrored(d, grain))) for plan in PLANS]
                for grain in range(GRAINS)
            ]
            for start, count, sources in runs(entries):
                value = result[:, grain_rows(start, count), head_cols(4 + j)]
                for plan, source in zip(PLANS, sources[1:]):
                    if source is not None:
                        other = result[:, grain_rows(source[1], count), head_cols(source[0] - HALF)]
                        value = jnp.where(send_plan[d][plan], other, value)
                pack[d, :, grain_rows(start, count), head_cols(j)] = value
            third(d, j).start()

    def take_back(h):
        for d in range(2):
            entries = [
                [mirrored_pair(d, result_place(plan, h, mirrored(d, grain))) for plan in PLANS]
                for grain in range(GRAINS)
            ]
            for start, count, sources in runs(entries):
                r = grain_rows(start, count)
                for plan, source in zip(PLANS, sources):
                    if source is None or (h >= 12 and plan != 8):
                        continue
                    take = returned[d][r] > 0.5
                    if h < 12:
                        take = take & recv_plan[d][plan]
                    for a in range(4):
                        other = late[d, a, grain_rows(source[1], count), head_cols(source[0])]
                        done[a, r, head_cols(h)] = jnp.where(take, other, done[a, r, head_cols(h)])

    early_slots = ((), (12,), (11, 10, 9, 8), (13,))
    for g in range(GROUPS):
        for d in range(2):
            first(d, g).wait_recv()
        for slot in early_slots[g]:
            pass_on(slot)

    complete = {4: 0, 5: 1, 6: 2, 7: 3}
    ready = {0: (0,), 1: (1,), 2: (2,), 3: (3,), 5: (4, 5), 6: (6, 8, 9, 11), 7: (7, 10)}

    def work(p, carry):
        h = jnp.where(p < 5, 12 - p, 8 + p)
        for d in range(2):
            second(d, h - HALF).wait_recv()

        @pl.when(p == 4)
        def _():
            pass_on(14)
            pass_on(15)

        three_tiles(h)
        for step in range(HALF):

            @pl.when(p == step)
            def _():
                if step in complete:
                    send_back(complete[step])
                for other in ready.get(step, ()):
                    gather_far(other)

        begin = jnp.where(p == 5, 4, p)
        end = jnp.where(p == 4, 4, jnp.where(p == 7, MOST, p + 1))
        lax.fori_loop(begin, end, lambda i, c: (five_tiles(i), c)[1], 0)
        return carry

    lax.fori_loop(0, HALF, work, 0)

    for j in range(BLOCKS):
        for d in range(2):
            third(d, j).wait_recv()
        take_back(12 + j)
        take_back(8 + j)

    for d in range(2):
        for g in range(GROUPS):
            first(d, g).wait_send()
        for s in range(HALF):
            second(d, s).wait_send()
        for j in range(BLOCKS):
            third(d, j).wait_send()


def write_out(done, att_ref, gq_ref, gk_ref, gv_ref, out_sem):
    copies = [
        pltpu.make_async_copy(done.at[a], ref, out_sem.at[a])
        for a, ref in enumerate((att_ref, gq_ref, gk_ref, gv_ref))
    ]
    for copy in copies:
        copy.start()
    for copy in copies:
        copy.wait()


def solution(mesh):
    n_dp, n_ctx = mesh.shape["dp"], mesh.shape["ctx"]
    token_spec = P(("dp", "ctx"), None)

    def body(queries, keys, values, grad_out, doc_ids, tile_pairs):
        width = queries.shape[1]
        in_hbm = pl.BlockSpec(memory_space=pltpu.HBM)
        low = jnp.bfloat16
        sem = pltpu.SemaphoreType.DMA
        held = [
            pltpu.with_memory_space_constraint(x, pltpu.HBM)
            for x in (queries, keys, values, grad_out, doc_ids.reshape(-1, TILE), tile_pairs.T)
        ]
        done = pl.pallas_call(
            functools.partial(kernel, n_dp, n_ctx),
            out_shape=jax.ShapeDtypeStruct((4, TILE, width), low),
            in_specs=[in_hbm] * 6,
            out_specs=pl.BlockSpec(memory_space=pltpu.VMEM),
            scratch_shapes=[
                pltpu.VMEM((4, TILE, width), low),
                pltpu.VMEM((2, 4, TILE, width), low),
                pltpu.VMEM((2, 4, TILE, HALF * HEAD), low),
                pltpu.VMEM((2, 4, TILE, MOST * HEAD), low),
                pltpu.VMEM((4, TILE, HALF * HEAD), low),
                pltpu.VMEM((2, 4, TILE, BLOCKS * HEAD), low),
                pltpu.VMEM((2, 4, TILE, BLOCKS * HEAD), low),
                pltpu.VMEM((3 * TILE, 3 * TILE), jnp.float32),
                pltpu.VMEM((2 * TILE, 2 * TILE), jnp.float32),
                pltpu.VMEM((2 * TILE, 2 * TILE), jnp.float32),
                pltpu.VMEM((TILE, TILE), low),
                pltpu.VMEM((2, TILE, TILE), jnp.float32),
                pltpu.VMEM((doc_ids.shape[0] // TILE, TILE), jnp.int32),
                pltpu.VMEM((2, tile_pairs.shape[0]), jnp.int32),
                sem((4,)),
                sem((2,)),
                sem((2, GROUPS)),
                sem((2, GROUPS)),
                sem((2, HALF)),
                sem((2, HALF)),
                sem((2, BLOCKS)),
                sem((2, BLOCKS)),
            ],
            compiler_params=pltpu.CompilerParams(
                collective_id=0, has_side_effects=True, vmem_limit_bytes=48 * 1024 * 1024
            ),
        )(*held)
        shape = jax.ShapeDtypeStruct(queries.shape, low)
        return pl.pallas_call(
            write_out,
            out_shape=(shape,) * 4,
            in_specs=[pl.BlockSpec(memory_space=pl.ANY)],
            out_specs=(in_hbm,) * 4,
            scratch_shapes=[sem((4,))],
            compiler_params=pltpu.CompilerParams(vmem_limit_bytes=1024 * 1024),
        )(done)

    return jax.shard_map(
        body,
        mesh=mesh,
        in_specs=(token_spec,) * 4 + (P(), P()),
        out_specs=(token_spec,) * 4,
        check_vma=False,
    )
```

```python
import functools
import math

import jax
import jax.numpy as jnp
from jax import lax
from jax.experimental import pallas as pl
from jax.experimental.pallas import tpu as pltpu
from jax.sharding import PartitionSpec as P

HEAD = 128
TILE = 128
HEADS = 16
HALF = 8
PER = 2
GROUPS = HALF // PER
WIDE = PER * HEAD
BLOCKS = 4
MOST = 12
GRAIN = 16
GRAINS = TILE // GRAIN
PLANS = (8, 10, 11, 12)
PIECE = {8: 8, 10: 4, 11: 3, 12: 2}
ORDER = {8: (12, 11, 10, 9, 8, 13, 14, 15), 10: (12, 11, 10, 13, 14), 11: (12, 11, 13, 14, 15), 12: (12, 13, 14)}
SCALE = 1.0 / math.sqrt(HEAD)
LOG2E = math.log2(math.e)
FAR = -1e30
MESH_ID = pl.DeviceIdType.MESH


def dot_nt(a, b):
    return lax.dot_general(a, b, (((1,), (1,)), ((), ())), preferred_element_type=jnp.float32)


def dot_nn(a, b):
    return lax.dot_general(a, b, (((1,), (0,)), ((), ())), preferred_element_type=jnp.float32)


def dot_tn(a, b):
    return lax.dot_general(a, b, (((0,), (0,)), ((), ())), preferred_element_type=jnp.float32)


def columns(start, size):
    return pl.ds(pl.multiple_of(start, HEAD), size)


def head_cols(h):
    return slice(h * HEAD, (h + 1) * HEAD)


def grain_rows(start, count):
    return slice(start * GRAIN, (start + count) * GRAIN)


def piece_grain(d, plan, t):
    return GRAINS - PIECE[plan] + t if d == 0 else t


def piece_place(plan, h, t):
    place = h * PIECE[plan] + t
    return ORDER[plan][place // GRAINS], place % GRAINS


def relay_source(d, plan, slot, grain):
    if slot not in ORDER[plan]:
        return None
    place = ORDER[plan].index(slot) * GRAINS + grain
    h, t = place // PIECE[plan], place % PIECE[plan]
    return (h, piece_grain(d, plan, t)) if h < plan else None


def relay_target(d, plan, h, grain):
    if h >= plan:
        return None
    t = grain - piece_grain(d, plan, 0)
    return piece_place(plan, h, t) if 0 <= t < PIECE[plan] else None


def result_place(plan, h, grain):
    if h >= 12:
        return (h - 12, grain)
    if plan == 8 and grain < 4:
        return (h - 8, grain + 4)
    if plan == 10 and h >= 10 and grain < 5:
        return (2 * (h - 10) + grain // 3, 5 + grain % 3)
    if plan == 11 and h == 11 and grain < 6:
        return (grain // 2, 6 + grain % 2)
    return None


def result_source(plan, block, grain):
    for h in range(8, 12):
        for g in range(GRAINS):
            if result_place(plan, h, g) == (block, grain):
                return (h, g)
    return None


def mirrored(d, grain):
    return grain if d == 0 else GRAINS - 1 - grain


def mirrored_pair(d, pair):
    return None if pair is None else (pair[0], mirrored(d, pair[1]))


def runs(entries):
    start = 0
    for at in range(1, GRAINS + 1):
        joined = at < GRAINS and all(
            (a is None and b is None) or (a is not None and b is not None and a[0] == b[0] and b[1] == a[1] + 1)
            for a, b in zip(entries[at - 1], entries[at])
        )
        if not joined:
            yield start, at - start, entries[start]
            start = at


def kernel(
    n_dp, n_ctx,
    q_ref, k_ref, v_ref, g_ref, ids_hbm, pairs_hbm,
    done,
    own, near, stage, far, result, pack, late, mask_wide, mask_left, mask_right, from_right, row_kind, ids_ref, pairs_ref,
    own_sem, side_sem, e1_send, e1_recv, e2_send, e2_recv, late_send, late_recv,
):
    n = n_dp * n_ctx
    me = lax.axis_index("dp") * n_ctx + lax.axis_index("ctx")
    right = lax.rem(me + 1, n)
    left = lax.rem(me + n - 1, n)
    target = [(x // n_ctx, lax.rem(x, n_ctx)) for x in (right, left)]
    inputs = (q_ref, k_ref, v_ref, g_ref)

    def own_copy(a):
        return pltpu.make_async_copy(inputs[a], own.at[a], own_sem.at[a])

    side_copies = [
        pltpu.make_async_copy(ids_hbm, ids_ref, side_sem.at[0]),
        pltpu.make_async_copy(pairs_hbm, pairs_ref, side_sem.at[1]),
    ]

    def first(d, g):
        cols = columns(g * WIDE, WIDE)
        return pltpu.make_async_remote_copy(
            src_ref=own.at[:, :, cols], dst_ref=near.at[d, :, :, cols],
            send_sem=e1_send.at[d, g], recv_sem=e1_recv.at[d, g],
            device_id=target[d], device_id_type=MESH_ID,
        )

    def second(d, s):
        return pltpu.make_async_remote_copy(
            src_ref=stage.at[d, :, :, columns(s * HEAD, HEAD)],
            dst_ref=near.at[d, :, :, columns((HALF + s) * HEAD, HEAD)],
            send_sem=e2_send.at[d, s], recv_sem=e2_recv.at[d, s],
            device_id=target[d], device_id_type=MESH_ID,
        )

    def third(d, j):
        cols = columns(j * HEAD, HEAD)
        return pltpu.make_async_remote_copy(
            src_ref=pack.at[d, :, :, cols], dst_ref=late.at[d, :, :, cols],
            send_sem=late_send.at[d, j], recv_sem=late_recv.at[d, j],
            device_id=target[d], device_id_type=MESH_ID,
        )

    barrier = pltpu.get_barrier_semaphore()
    for d in range(2):
        pl.semaphore_signal(barrier, inc=1, device_id=target[d], device_id_type=MESH_ID)
    for copy in side_copies:
        copy.start()
    for a in range(4):
        own_copy(a).start()
    pl.semaphore_wait(barrier, 2)
    for a in range(4):
        own_copy(a).wait()
    for g in range(GROUPS):
        for d in range(2):
            first(d, g).start()

    for copy in side_copies:
        copy.wait()
    tiles = [lax.rem(me + n + t, n) for t in range(-2, 3)]
    rows = [ids_ref[pl.ds(t, 1), :].astype(jnp.float32) for t in tiles]
    eye = lax.broadcasted_iota(jnp.int32, (TILE, TILE), 0) == lax.broadcasted_iota(jnp.int32, (TILE, TILE), 1)

    def upright(row):
        return jnp.sum(jnp.where(eye, jnp.broadcast_to(row, (TILE, TILE)), 0.0), axis=1, keepdims=True)

    def middle(t):
        before = rows[t - 1][:, TILE - 1 :]
        head, tail = rows[t][:, :1], rows[t][:, TILE - 1 :]
        after = rows[t + 1][:, :1]
        return (before == head) & (head == tail) & (tail == after)

    def plans_of(middle_tile, far_tile):
        count = jnp.sum(jnp.where(rows[far_tile] == rows[middle_tile][:, :1], 1.0, 0.0), axis=1, keepdims=True)
        return {12: count < 33, 11: (count > 32) & (count < 49), 10: (count > 48) & (count < 65), 8: count > 64}

    mid_left, mid_own, mid_right = middle(1), middle(2), middle(3)
    send_plan = [{p: c & mid_own for p, c in plans_of(2, f).items()} for f in (1, 3)]
    recv_plan = [plans_of(1, 0), plans_of(3, 4)]
    codes = pairs_ref[0:1, :] * n + pairs_ref[1:2, :]

    def is_listed(x, y):
        hit = (codes == tiles[x] * n + tiles[y]) | (codes == tiles[y] * n + tiles[x])
        return jnp.max(jnp.where(hit, 1.0, 0.0), axis=1, keepdims=True)

    up = [upright(r) for r in rows]
    flags = {}
    for x in range(5):
        for y in range(x, min(x + 3, 5)):
            flags[x, y] = is_listed(x, y)
            flags[y, x] = flags[x, y]

    def number(condition):
        return jnp.where(condition, 1.0, 0.0)

    def plain(x):
        return rows[x], up[x], [(x, None, None)]

    def mixed(x, y, along, across):
        return (
            jnp.where(along > 0.5, rows[x], rows[y]),
            jnp.where(across > 0.5, up[x], up[y]),
            [(x, along, across), (y, 1.0 - along, 1.0 - across)],
        )

    def mask_of(query_tile, key_tile, keep=None):
        listed = jnp.zeros((TILE, TILE), jnp.float32)
        for x, _, across in query_tile[2]:
            for y, along, _ in key_tile[2]:
                if (x, y) in flags:
                    share = jnp.broadcast_to(flags[x, y], (TILE, TILE))
                    share = share if across is None else share * across
                    listed += share if along is None else share * along
        if keep is not None:
            listed = listed * keep
        return jnp.where((query_tile[1] == key_tile[0]) & (listed > 0.5), 0.0, FAR)

    far_left = [number((r[0] == rows[1][:, :1]) & mid_left) for r in (rows, up)]
    far_right = [number((r[4] == rows[3][:, :1]) & mid_right) for r in (rows, up)]
    take_right = [number((r[1] != rows[2][:, :1]) & mid_own) for r in (rows, up)]
    far_rows = (far_left[1], far_right[1])
    centre = plain(2)
    after = plain(3)
    near_side = mixed(3, 1, *take_right)
    left_side = mixed(0, 2, *far_left)
    right_side = mixed(4, 2, *far_right)
    one, two, three = slice(0, TILE), slice(TILE, 2 * TILE), slice(2 * TILE, 3 * TILE)
    not_middle = 1.0 - number(mid_own)
    mask_wide[one, one] = mask_of(near_side, near_side)
    mask_wide[one, two] = mask_of(near_side, centre)
    mask_wide[two, one] = mask_of(centre, near_side)
    mask_wide[two, two] = mask_of(centre, centre)
    mask_wide[two, three] = mask_of(centre, after, not_middle)
    mask_wide[three, two] = mask_of(after, centre, not_middle)
    mask_wide[three, three] = mask_of(after, after)
    for ref, x, y in ((mask_left, left_side, near_side), (mask_right, right_side, after)):
        ref[one, one] = mask_of(x, x)
        ref[one, two] = mask_of(x, y)
        ref[two, one] = mask_of(y, x)
        ref[two, two] = mask_of(y, y)
    square = (TILE, TILE)
    from_right[...] = jnp.broadcast_to(take_right[1], square).astype(jnp.bfloat16)
    reaches_left = number(up[2] == rows[1][:, TILE - 1 :])
    reaches_right = number(up[2] == rows[3][:, :1])
    row_kind[0] = jnp.broadcast_to(reaches_left, square)
    row_kind[1] = jnp.broadcast_to(reaches_right, square)
    returned = [reaches_left * number(mid_left), reaches_right * number(mid_right)]

    def pass_on(slot):
        for d in range(2):
            entries = [
                [(slot, grain)] + [relay_source(d, plan, slot, grain) for plan in PLANS] for grain in range(GRAINS)
            ]
            for start, count, sources in runs(entries):
                value = own[:, grain_rows(start, count), head_cols(slot)]
                for plan, source in zip(PLANS, sources[1:]):
                    if source is not None:
                        other = near[d, :, grain_rows(source[1], count), head_cols(source[0])]
                        value = jnp.where(send_plan[d][plan], other, value)
                stage[d, :, grain_rows(start, count), head_cols(slot - HALF)] = value
            second(d, slot - HALF).start()

    def gather_far(h):
        for d in range(2):
            entries = [
                [relay_target(d, plan, h, grain) or (None if plan != 8 else (8, grain)) for plan in PLANS]
                for grain in range(GRAINS)
            ]
            for start, count, sources in runs(entries):
                value = None
                for plan, source in zip(PLANS, sources):
                    if source is not None:
                        other = near[d, :, grain_rows(source[1], count), head_cols(source[0])]
                        value = other if value is None else jnp.where(recv_plan[d][plan], other, value)
                r = grain_rows(start, count)
                for a in range(4):
                    far[d, a, r, head_cols(h)] = jnp.where(far_rows[d][r] > 0.5, value[a], own[a, r, head_cols(h)])

    def softmax_parts(query, grads, keys, values, mask):
        scores = dot_nt(query, keys) * (SCALE * LOG2E) + mask
        top = jnp.max(scores, axis=1, keepdims=True)
        weights = jnp.exp2(scores - top)
        inverse = 1.0 / jnp.sum(weights, axis=1, keepdims=True)
        dprobs = dot_nt(grads, values)
        delta = jnp.sum(weights * dprobs, axis=1, keepdims=True) * inverse
        return weights, inverse, dprobs, delta

    def load(h):
        at = columns(h * HEAD, HEAD)
        after_rows = [near[1, a, :, at] for a in range(4)]
        use_right = from_right[...] > 0.5
        near_rows = [jnp.where(use_right, after_rows[a], near[0, a, :, at]) for a in range(4)]
        return at, near_rows, [own[a, :, at] for a in range(4)], after_rows

    def stacked(*parts):
        return [jnp.concatenate(part, axis=0) for part in zip(*parts)]

    def full(parts):
        weights, inverse, dprobs, delta = parts
        p = weights * inverse
        return p.astype(jnp.bfloat16), (p * (dprobs - delta)).astype(jnp.bfloat16)

    def partial(parts, cols):
        weights, inverse, dprobs, delta = parts
        p = weights[:, cols] * inverse
        return p.astype(jnp.bfloat16), (p * (dprobs[:, cols] - delta)).astype(jnp.bfloat16)

    def three_tiles(h):
        at, near_rows, own_rows, after_rows = load(h)
        back = columns((h - HALF) * HEAD, HEAD)
        q, k, v, g = stacked(near_rows, own_rows, after_rows)
        wide = slice(0, 2 * TILE)
        p_near, ds_near = full(softmax_parts(q[one], g[one], k[wide], v[wide], mask_wide[one, wide]))
        p_own, ds_own = full(softmax_parts(q[two], g[two], k, v, mask_wide[two, :]))
        tail = slice(TILE, 3 * TILE)
        p_after, ds_after = partial(softmax_parts(q[three], g[three], k[tail], v[tail], mask_wide[three, tail]), one)
        result[0, :, back] = dot_nn(p_near, v[wide]).astype(jnp.bfloat16)
        result[1, :, back] = (dot_nn(ds_near, k[wide]) * SCALE).astype(jnp.bfloat16)
        result[2, :, back] = (
            dot_tn(jnp.concatenate([ds_near[:, one], ds_own[:, one]], axis=0), q[wide]) * SCALE
        ).astype(jnp.bfloat16)
        result[3, :, back] = dot_tn(
            jnp.concatenate([p_near[:, one], p_own[:, one]], axis=0), g[wide]
        ).astype(jnp.bfloat16)
        done[0, :, at] = dot_nn(p_own, v).astype(jnp.bfloat16)
        done[1, :, at] = (dot_nn(ds_own, k) * SCALE).astype(jnp.bfloat16)
        done[2, :, at] = (
            dot_tn(jnp.concatenate([ds_near[:, two], ds_own[:, two], ds_after], axis=0), q) * SCALE
        ).astype(jnp.bfloat16)
        done[3, :, at] = dot_tn(
            jnp.concatenate([p_near[:, two], p_own[:, two], p_after], axis=0), g
        ).astype(jnp.bfloat16)

    def two_tiles(first_rows, second_rows, mask):
        q, k, v, g = stacked(first_rows, second_rows)
        p_one, ds_one = full(softmax_parts(q[one], g[one], k, v, mask[one, :]))
        p_two, ds_two = partial(softmax_parts(q[two], g[two], k, v, mask[two, :]), one)
        return (
            dot_nn(p_one, v),
            dot_nn(ds_one, k) * SCALE,
            dot_tn(jnp.concatenate([ds_one[:, one], ds_two], axis=0), q) * SCALE,
            dot_tn(jnp.concatenate([p_one[:, one], p_two], axis=0), g),
        )

    def five_tiles(h, known=False):
        at, near_rows, own_rows, after_rows = load(h)
        far_sides = [[far[d, a, :, at] for a in range(4)] for d in range(2)]
        before = two_tiles(far_sides[0], near_rows, mask_left)
        behind = two_tiles(far_sides[1], after_rows, mask_right)
        if known:
            inside = [done[a, :, at].astype(jnp.float32) for a in range(4)]
        else:
            q, k, v, g = own_rows
            p, ds = full(softmax_parts(q, g, k, v, mask_wide[two, two]))
            inside = (dot_nn(p, v), dot_nn(ds, k) * SCALE, dot_tn(ds, q) * SCALE, dot_tn(p, g))
        on_left, on_right = row_kind[0] > 0.5, row_kind[1] > 0.5
        for a in range(4):
            value = jnp.where(on_left, before[a], jnp.where(on_right, behind[a], inside[a]))
            done[a, :, at] = value.astype(jnp.bfloat16)

    def send_back(j):
        for d in range(2):
            entries = [
                [(12 + j, grain)]
                + [mirrored_pair(d, result_source(plan, j, mirrored(d, grain))) for plan in PLANS]
                for grain in range(GRAINS)
            ]
            for start, count, sources in runs(entries):
                value = result[:, grain_rows(start, count), head_cols(4 + j)]
                for plan, source in zip(PLANS, sources[1:]):
                    if source is not None:
                        other = result[:, grain_rows(source[1], count), head_cols(source[0] - HALF)]
                        value = jnp.where(send_plan[d][plan], other, value)
                pack[d, :, grain_rows(start, count), head_cols(j)] = value
            third(d, j).start()

    def take_back(h):
        for d in range(2):
            entries = [
                [mirrored_pair(d, result_place(plan, h, mirrored(d, grain))) for plan in PLANS]
                for grain in range(GRAINS)
            ]
            for start, count, sources in runs(entries):
                r = grain_rows(start, count)
                for plan, source in zip(PLANS, sources):
                    if source is None or (h >= 12 and plan != 8):
                        continue
                    take = returned[d][r] > 0.5
                    if h < 12:
                        take = take & recv_plan[d][plan]
                    for a in range(4):
                        other = late[d, a, grain_rows(source[1], count), head_cols(source[0])]
                        done[a, r, head_cols(h)] = jnp.where(take, other, done[a, r, head_cols(h)])

    early_slots = ((), (12,), (11, 10, 9, 8), (13,))
    for g in range(GROUPS):
        for d in range(2):
            first(d, g).wait_recv()
        for slot in early_slots[g]:
            pass_on(slot)

    complete = {4: 0, 5: 1, 6: 2, 7: 3}
    ready = {0: (0,), 1: (1,), 2: (2,), 3: (3,), 5: (4, 5), 6: (6, 8, 9, 11), 7: (7, 10)}

    def work(p, carry):
        h = jnp.where(p < 5, 12 - p, 8 + p)
        for d in range(2):
            second(d, h - HALF).wait_recv()

        @pl.when(p == 4)
        def _():
            pass_on(14)
            pass_on(15)

        three_tiles(h)
        for step in range(HALF):

            @pl.when(p == step)
            def _():
                if step in complete:
                    send_back(complete[step])
                for other in ready.get(step, ()):
                    gather_far(other)

        begin = jnp.where(p == 5, 4, p)
        end = jnp.where(p == 4, 4, p + 1)
        lax.fori_loop(begin, end, lambda i, c: (five_tiles(i), c)[1], 0)
        return carry

    lax.fori_loop(0, HALF, work, 0)
    lax.fori_loop(HALF, MOST, lambda h, c: (five_tiles(h, True), c)[1], 0)

    for j in range(BLOCKS):
        for d in range(2):
            third(d, j).wait_recv()
        take_back(12 + j)
        take_back(8 + j)

    for d in range(2):
        for g in range(GROUPS):
            first(d, g).wait_send()
        for s in range(HALF):
            second(d, s).wait_send()
        for j in range(BLOCKS):
            third(d, j).wait_send()


def write_out(done, att_ref, gq_ref, gk_ref, gv_ref, out_sem):
    copies = [
        pltpu.make_async_copy(done.at[a], ref, out_sem.at[a])
        for a, ref in enumerate((att_ref, gq_ref, gk_ref, gv_ref))
    ]
    for copy in copies:
        copy.start()
    for copy in copies:
        copy.wait()


def solution(mesh):
    n_dp, n_ctx = mesh.shape["dp"], mesh.shape["ctx"]
    token_spec = P(("dp", "ctx"), None)

    def body(queries, keys, values, grad_out, doc_ids, tile_pairs):
        width = queries.shape[1]
        in_hbm = pl.BlockSpec(memory_space=pltpu.HBM)
        low = jnp.bfloat16
        sem = pltpu.SemaphoreType.DMA
        held = [
            pltpu.with_memory_space_constraint(x, pltpu.HBM)
            for x in (queries, keys, values, grad_out, doc_ids.reshape(-1, TILE), tile_pairs.T)
        ]
        done = pl.pallas_call(
            functools.partial(kernel, n_dp, n_ctx),
            out_shape=jax.ShapeDtypeStruct((4, TILE, width), low),
            in_specs=[in_hbm] * 6,
            out_specs=pl.BlockSpec(memory_space=pltpu.VMEM),
            scratch_shapes=[
                pltpu.VMEM((4, TILE, width), low),
                pltpu.VMEM((2, 4, TILE, width), low),
                pltpu.VMEM((2, 4, TILE, HALF * HEAD), low),
                pltpu.VMEM((2, 4, TILE, MOST * HEAD), low),
                pltpu.VMEM((4, TILE, HALF * HEAD), low),
                pltpu.VMEM((2, 4, TILE, BLOCKS * HEAD), low),
                pltpu.VMEM((2, 4, TILE, BLOCKS * HEAD), low),
                pltpu.VMEM((3 * TILE, 3 * TILE), jnp.float32),
                pltpu.VMEM((2 * TILE, 2 * TILE), jnp.float32),
                pltpu.VMEM((2 * TILE, 2 * TILE), jnp.float32),
                pltpu.VMEM((TILE, TILE), low),
                pltpu.VMEM((2, TILE, TILE), jnp.float32),
                pltpu.VMEM((doc_ids.shape[0] // TILE, TILE), jnp.int32),
                pltpu.VMEM((2, tile_pairs.shape[0]), jnp.int32),
                sem((4,)),
                sem((2,)),
                sem((2, GROUPS)),
                sem((2, GROUPS)),
                sem((2, HALF)),
                sem((2, HALF)),
                sem((2, BLOCKS)),
                sem((2, BLOCKS)),
            ],
            compiler_params=pltpu.CompilerParams(
                collective_id=0, has_side_effects=True, vmem_limit_bytes=48 * 1024 * 1024
            ),
        )(*held)
        shape = jax.ShapeDtypeStruct(queries.shape, low)
        return pl.pallas_call(
            write_out,
            out_shape=(shape,) * 4,
            in_specs=[pl.BlockSpec(memory_space=pl.ANY)],
            out_specs=(in_hbm,) * 4,
            scratch_shapes=[sem((4,))],
            compiler_params=pltpu.CompilerParams(vmem_limit_bytes=1024 * 1024),
        )(done)

    return jax.shard_map(
        body,
        mesh=mesh,
        in_specs=(token_spec,) * 4 + (P(), P()),
        out_specs=(token_spec,) * 4,
        check_vma=False,
    )
```

```python
import functools
import math

import jax
import jax.numpy as jnp
from jax import lax
from jax.experimental import pallas as pl
from jax.experimental.pallas import tpu as pltpu
from jax.sharding import PartitionSpec as P

HEAD = 128
TILE = 128
HEADS = 16
HALF = 8
PER = 2
GROUPS = HALF // PER
WIDE = PER * HEAD
BLOCKS = 4
MOST = 12
GRAIN = 16
GRAINS = TILE // GRAIN
PLANS = (8, 10, 11, 12)
PIECE = {8: 8, 10: 4, 11: 3, 12: 2}
ORDER = {8: (12, 11, 10, 9, 8, 13, 14, 15), 10: (12, 11, 10, 13, 15), 11: (12, 11, 13, 15, 14), 12: (12, 13, 15)}
SCALE = 1.0 / math.sqrt(HEAD)
LOG2E = math.log2(math.e)
FAR = -1e30
MESH_ID = pl.DeviceIdType.MESH


def dot_nt(a, b):
    return lax.dot_general(a, b, (((1,), (1,)), ((), ())), preferred_element_type=jnp.float32)


def dot_nn(a, b):
    return lax.dot_general(a, b, (((1,), (0,)), ((), ())), preferred_element_type=jnp.float32)


def dot_tn(a, b):
    return lax.dot_general(a, b, (((0,), (0,)), ((), ())), preferred_element_type=jnp.float32)


def columns(start, size):
    return pl.ds(pl.multiple_of(start, HEAD), size)


def head_cols(h):
    return slice(h * HEAD, (h + 1) * HEAD)


def grain_rows(start, count):
    return slice(start * GRAIN, (start + count) * GRAIN)


def piece_grain(d, plan, t):
    return GRAINS - PIECE[plan] + t if d == 0 else t


def piece_place(plan, h, t):
    place = h * PIECE[plan] + t
    return ORDER[plan][place // GRAINS], place % GRAINS


def relay_source(d, plan, slot, grain):
    if slot not in ORDER[plan]:
        return None
    place = ORDER[plan].index(slot) * GRAINS + grain
    h, t = place // PIECE[plan], place % PIECE[plan]
    return (h, piece_grain(d, plan, t)) if h < plan else None


def relay_target(d, plan, h, grain):
    if h >= plan:
        return None
    t = grain - piece_grain(d, plan, 0)
    return piece_place(plan, h, t) if 0 <= t < PIECE[plan] else None


def result_place(plan, h, grain):
    if h >= 12:
        return (h - 12, grain)
    if plan == 8 and grain < 4:
        return (h - 8, grain + 4)
    if plan == 10 and h >= 10 and grain < 5:
        return (2 * (h - 10) + grain // 3, 5 + grain % 3)
    if plan == 11 and h == 11 and grain < 6:
        return (grain // 2, 6 + grain % 2)
    return None


def result_source(plan, block, grain):
    for h in range(8, 12):
        for g in range(GRAINS):
            if result_place(plan, h, g) == (block, grain):
                return (h, g)
    return None


def mirrored(d, grain):
    return grain if d == 0 else GRAINS - 1 - grain


def mirrored_pair(d, pair):
    return None if pair is None else (pair[0], mirrored(d, pair[1]))


def runs(entries):
    start = 0
    for at in range(1, GRAINS + 1):
        joined = at < GRAINS and all(
            (a is None and b is None) or (a is not None and b is not None and a[0] == b[0] and b[1] == a[1] + 1)
            for a, b in zip(entries[at - 1], entries[at])
        )
        if not joined:
            yield start, at - start, entries[start]
            start = at


def kernel(
    n_dp, n_ctx,
    q_ref, k_ref, v_ref, g_ref, ids_hbm, pairs_hbm,
    done,
    own, near, stage, far, result, pack, late, mask_wide, mask_left, mask_right, from_right, row_kind, ids_ref, pairs_ref,
    own_sem, side_sem, e1_send, e1_recv, e2_send, e2_recv, late_send, late_recv,
):
    n = n_dp * n_ctx
    me = lax.axis_index("dp") * n_ctx + lax.axis_index("ctx")
    right = lax.rem(me + 1, n)
    left = lax.rem(me + n - 1, n)
    target = [(x // n_ctx, lax.rem(x, n_ctx)) for x in (right, left)]
    inputs = (q_ref, k_ref, v_ref, g_ref)

    def own_copy(a):
        return pltpu.make_async_copy(inputs[a], own.at[a], own_sem.at[a])

    side_copies = [
        pltpu.make_async_copy(ids_hbm, ids_ref, side_sem.at[0]),
        pltpu.make_async_copy(pairs_hbm, pairs_ref, side_sem.at[1]),
    ]

    def first(d, g):
        cols = columns(g * WIDE, WIDE)
        return pltpu.make_async_remote_copy(
            src_ref=own.at[:, :, cols], dst_ref=near.at[d, :, :, cols],
            send_sem=e1_send.at[d, g], recv_sem=e1_recv.at[d, g],
            device_id=target[d], device_id_type=MESH_ID,
        )

    def second(d, s):
        return pltpu.make_async_remote_copy(
            src_ref=stage.at[d, :, :, columns(s * HEAD, HEAD)],
            dst_ref=near.at[d, :, :, columns((HALF + s) * HEAD, HEAD)],
            send_sem=e2_send.at[d, s], recv_sem=e2_recv.at[d, s],
            device_id=target[d], device_id_type=MESH_ID,
        )

    def third(d, j):
        cols = columns(j * HEAD, HEAD)
        return pltpu.make_async_remote_copy(
            src_ref=pack.at[d, :, :, cols], dst_ref=late.at[d, :, :, cols],
            send_sem=late_send.at[d, j], recv_sem=late_recv.at[d, j],
            device_id=target[d], device_id_type=MESH_ID,
        )

    barrier = pltpu.get_barrier_semaphore()
    for d in range(2):
        pl.semaphore_signal(barrier, inc=1, device_id=target[d], device_id_type=MESH_ID)
    for copy in side_copies:
        copy.start()
    for a in range(4):
        own_copy(a).start()
    pl.semaphore_wait(barrier, 2)
    for a in range(4):
        own_copy(a).wait()
    for g in range(GROUPS):
        for d in range(2):
            first(d, g).start()

    for copy in side_copies:
        copy.wait()
    tiles = [lax.rem(me + n + t, n) for t in range(-2, 3)]
    rows = [ids_ref[pl.ds(t, 1), :].astype(jnp.float32) for t in tiles]
    eye = lax.broadcasted_iota(jnp.int32, (TILE, TILE), 0) == lax.broadcasted_iota(jnp.int32, (TILE, TILE), 1)

    def upright(row):
        return jnp.sum(jnp.where(eye, jnp.broadcast_to(row, (TILE, TILE)), 0.0), axis=1, keepdims=True)

    def middle(t):
        before = rows[t - 1][:, TILE - 1 :]
        head, tail = rows[t][:, :1], rows[t][:, TILE - 1 :]
        after = rows[t + 1][:, :1]
        return (before == head) & (head == tail) & (tail == after)

    def plans_of(middle_tile, far_tile):
        count = jnp.sum(jnp.where(rows[far_tile] == rows[middle_tile][:, :1], 1.0, 0.0), axis=1, keepdims=True)
        return {12: count < 33, 11: (count > 32) & (count < 49), 10: (count > 48) & (count < 65), 8: count > 64}

    mid_left, mid_own, mid_right = middle(1), middle(2), middle(3)
    send_plan = [{p: c & mid_own for p, c in plans_of(2, f).items()} for f in (1, 3)]
    recv_plan = [plans_of(1, 0), plans_of(3, 4)]
    codes = pairs_ref[0:1, :] * n + pairs_ref[1:2, :]

    def is_listed(x, y):
        hit = (codes == tiles[x] * n + tiles[y]) | (codes == tiles[y] * n + tiles[x])
        return jnp.max(jnp.where(hit, 1.0, 0.0), axis=1, keepdims=True)

    up = [upright(r) for r in rows]
    flags = {}
    for x in range(5):
        for y in range(x, min(x + 3, 5)):
            flags[x, y] = is_listed(x, y)
            flags[y, x] = flags[x, y]

    def number(condition):
        return jnp.where(condition, 1.0, 0.0)

    def plain(x):
        return rows[x], up[x], [(x, None, None)]

    def mixed(x, y, along, across):
        return (
            jnp.where(along > 0.5, rows[x], rows[y]),
            jnp.where(across > 0.5, up[x], up[y]),
            [(x, along, across), (y, 1.0 - along, 1.0 - across)],
        )

    def mask_of(query_tile, key_tile, keep=None):
        listed = jnp.zeros((TILE, TILE), jnp.float32)
        for x, _, across in query_tile[2]:
            for y, along, _ in key_tile[2]:
                if (x, y) in flags:
                    share = jnp.broadcast_to(flags[x, y], (TILE, TILE))
                    share = share if across is None else share * across
                    listed += share if along is None else share * along
        if keep is not None:
            listed = listed * keep
        return jnp.where((query_tile[1] == key_tile[0]) & (listed > 0.5), 0.0, FAR)

    far_left = [number((r[0] == rows[1][:, :1]) & mid_left) for r in (rows, up)]
    far_right = [number((r[4] == rows[3][:, :1]) & mid_right) for r in (rows, up)]
    take_right = [number((r[1] != rows[2][:, :1]) & mid_own) for r in (rows, up)]
    far_rows = (far_left[1], far_right[1])
    centre = plain(2)
    after = plain(3)
    near_side = mixed(3, 1, *take_right)
    left_side = mixed(0, 2, *far_left)
    right_side = mixed(4, 2, *far_right)
    one, two, three = slice(0, TILE), slice(TILE, 2 * TILE), slice(2 * TILE, 3 * TILE)
    not_middle = 1.0 - number(mid_own)
    mask_wide[one, one] = mask_of(near_side, near_side)
    mask_wide[one, two] = mask_of(near_side, centre)
    mask_wide[two, one] = mask_of(centre, near_side)
    mask_wide[two, two] = mask_of(centre, centre)
    mask_wide[two, three] = mask_of(centre, after, not_middle)
    mask_wide[three, two] = mask_of(after, centre, not_middle)
    mask_wide[three, three] = mask_of(after, after)
    for ref, x, y in ((mask_left, left_side, near_side), (mask_right, right_side, after)):
        ref[one, one] = mask_of(x, x)
        ref[one, two] = mask_of(x, y)
        ref[two, one] = mask_of(y, x)
        ref[two, two] = mask_of(y, y)
    square = (TILE, TILE)
    from_right[...] = jnp.broadcast_to(take_right[1], square).astype(jnp.bfloat16)
    reaches_left = number(up[2] == rows[1][:, TILE - 1 :])
    reaches_right = number(up[2] == rows[3][:, :1])
    row_kind[0] = jnp.broadcast_to(reaches_left, square)
    row_kind[1] = jnp.broadcast_to(reaches_right, square)
    returned = [reaches_left * number(mid_left), reaches_right * number(mid_right)]

    def pass_on(slot):
        for d in range(2):
            entries = [
                [(slot, grain)] + [relay_source(d, plan, slot, grain) for plan in PLANS] for grain in range(GRAINS)
            ]
            for start, count, sources in runs(entries):
                value = own[:, grain_rows(start, count), head_cols(slot)]
                for plan, source in zip(PLANS, sources[1:]):
                    if source is not None:
                        other = near[d, :, grain_rows(source[1], count), head_cols(source[0])]
                        value = jnp.where(send_plan[d][plan], other, value)
                stage[d, :, grain_rows(start, count), head_cols(slot - HALF)] = value
            second(d, slot - HALF).start()

    def gather_far(h):
        for d in range(2):
            entries = [
                [relay_target(d, plan, h, grain) or (None if plan != 8 else (8, grain)) for plan in PLANS]
                for grain in range(GRAINS)
            ]
            for start, count, sources in runs(entries):
                value = None
                for plan, source in zip(PLANS, sources):
                    if source is not None:
                        other = near[d, :, grain_rows(source[1], count), head_cols(source[0])]
                        value = other if value is None else jnp.where(recv_plan[d][plan], other, value)
                r = grain_rows(start, count)
                for a in range(4):
                    far[d, a, r, head_cols(h)] = jnp.where(far_rows[d][r] > 0.5, value[a], own[a, r, head_cols(h)])

    def softmax_parts(query, grads, keys, values, mask):
        scores = dot_nt(query, keys) * (SCALE * LOG2E) + mask
        top = jnp.max(scores, axis=1, keepdims=True)
        weights = jnp.exp2(scores - top)
        inverse = 1.0 / jnp.sum(weights, axis=1, keepdims=True)
        dprobs = dot_nt(grads, values)
        delta = jnp.sum(weights * dprobs, axis=1, keepdims=True) * inverse
        return weights, inverse, dprobs, delta

    def load(h):
        at = columns(h * HEAD, HEAD)
        after_rows = [near[1, a, :, at] for a in range(4)]
        use_right = from_right[...] > 0.5
        near_rows = [jnp.where(use_right, after_rows[a], near[0, a, :, at]) for a in range(4)]
        return at, near_rows, [own[a, :, at] for a in range(4)], after_rows

    def stacked(*parts):
        return [jnp.concatenate(part, axis=0) for part in zip(*parts)]

    def full(parts):
        weights, inverse, dprobs, delta = parts
        p = weights * inverse
        return p.astype(jnp.bfloat16), (p * (dprobs - delta)).astype(jnp.bfloat16)

    def partial(parts, cols):
        weights, inverse, dprobs, delta = parts
        p = weights[:, cols] * inverse
        return p.astype(jnp.bfloat16), (p * (dprobs[:, cols] - delta)).astype(jnp.bfloat16)

    def three_tiles(h):
        at, near_rows, own_rows, after_rows = load(h)
        back = columns((h - HALF) * HEAD, HEAD)
        q, k, v, g = stacked(near_rows, own_rows, after_rows)
        wide = slice(0, 2 * TILE)
        p_near, ds_near = full(softmax_parts(q[one], g[one], k[wide], v[wide], mask_wide[one, wide]))
        p_own, ds_own = full(softmax_parts(q[two], g[two], k, v, mask_wide[two, :]))
        tail = slice(TILE, 3 * TILE)
        p_after, ds_after = partial(softmax_parts(q[three], g[three], k[tail], v[tail], mask_wide[three, tail]), one)
        result[0, :, back] = dot_nn(p_near, v[wide]).astype(jnp.bfloat16)
        result[1, :, back] = (dot_nn(ds_near, k[wide]) * SCALE).astype(jnp.bfloat16)
        result[2, :, back] = (
            dot_tn(jnp.concatenate([ds_near[:, one], ds_own[:, one]], axis=0), q[wide]) * SCALE
        ).astype(jnp.bfloat16)
        result[3, :, back] = dot_tn(
            jnp.concatenate([p_near[:, one], p_own[:, one]], axis=0), g[wide]
        ).astype(jnp.bfloat16)
        done[0, :, at] = dot_nn(p_own, v).astype(jnp.bfloat16)
        done[1, :, at] = (dot_nn(ds_own, k) * SCALE).astype(jnp.bfloat16)
        done[2, :, at] = (
            dot_tn(jnp.concatenate([ds_near[:, two], ds_own[:, two], ds_after], axis=0), q) * SCALE
        ).astype(jnp.bfloat16)
        done[3, :, at] = dot_tn(
            jnp.concatenate([p_near[:, two], p_own[:, two], p_after], axis=0), g
        ).astype(jnp.bfloat16)

    def two_tiles(first_rows, second_rows, mask):
        q, k, v, g = stacked(first_rows, second_rows)
        p_one, ds_one = full(softmax_parts(q[one], g[one], k, v, mask[one, :]))
        p_two, ds_two = partial(softmax_parts(q[two], g[two], k, v, mask[two, :]), one)
        return (
            dot_nn(p_one, v),
            dot_nn(ds_one, k) * SCALE,
            dot_tn(jnp.concatenate([ds_one[:, one], ds_two], axis=0), q) * SCALE,
            dot_tn(jnp.concatenate([p_one[:, one], p_two], axis=0), g),
        )

    def five_tiles(h, known=False):
        at, near_rows, own_rows, after_rows = load(h)
        far_sides = [[far[d, a, :, at] for a in range(4)] for d in range(2)]
        before = two_tiles(far_sides[0], near_rows, mask_left)
        behind = two_tiles(far_sides[1], after_rows, mask_right)
        if known:
            inside = [done[a, :, at].astype(jnp.float32) for a in range(4)]
        else:
            q, k, v, g = own_rows
            p, ds = full(softmax_parts(q, g, k, v, mask_wide[two, two]))
            inside = (dot_nn(p, v), dot_nn(ds, k) * SCALE, dot_tn(ds, q) * SCALE, dot_tn(p, g))
        on_left, on_right = row_kind[0] > 0.5, row_kind[1] > 0.5
        for a in range(4):
            value = jnp.where(on_left, before[a], jnp.where(on_right, behind[a], inside[a]))
            done[a, :, at] = value.astype(jnp.bfloat16)

    def send_back(j):
        for d in range(2):
            entries = [
                [(12 + j, grain)]
                + [mirrored_pair(d, result_source(plan, j, mirrored(d, grain))) for plan in PLANS]
                for grain in range(GRAINS)
            ]
            for start, count, sources in runs(entries):
                value = result[:, grain_rows(start, count), head_cols(4 + j)]
                for plan, source in zip(PLANS, sources[1:]):
                    if source is not None:
                        other = result[:, grain_rows(source[1], count), head_cols(source[0] - HALF)]
                        value = jnp.where(send_plan[d][plan], other, value)
                pack[d, :, grain_rows(start, count), head_cols(j)] = value
            third(d, j).start()

    def take_back(h):
        for d in range(2):
            entries = [
                [mirrored_pair(d, result_place(plan, h, mirrored(d, grain))) for plan in PLANS]
                for grain in range(GRAINS)
            ]
            for start, count, sources in runs(entries):
                r = grain_rows(start, count)
                for plan, source in zip(PLANS, sources):
                    if source is None or (h >= 12 and plan != 8):
                        continue
                    take = returned[d][r] > 0.5
                    if h < 12:
                        take = take & recv_plan[d][plan]
                    for a in range(4):
                        other = late[d, a, grain_rows(source[1], count), head_cols(source[0])]
                        done[a, r, head_cols(h)] = jnp.where(take, other, done[a, r, head_cols(h)])

    early_slots = ((), (12,), (11, 10, 9, 8), (13,))
    for g in range(GROUPS):
        for d in range(2):
            first(d, g).wait_recv()
        for slot in early_slots[g]:
            pass_on(slot)

    complete = {4: 0, 5: 1, 6: 2, 7: 3}
    ready = {0: (0,), 1: (1,), 2: (2,), 3: (3,), 5: (4, 5), 6: (6,), 7: (7, 8, 9, 10, 11)}

    def work(p, carry):
        h = jnp.where(p < 5, 12 - p, 8 + p)
        for d in range(2):
            second(d, h - HALF).wait_recv()

        @pl.when(p == 2)
        def _():
            pass_on(14)

        @pl.when(p == 4)
        def _():
            pass_on(15)

        three_tiles(h)
        for step in range(HALF):

            @pl.when(p == step)
            def _():
                if step in complete:
                    send_back(complete[step])
                for other in ready.get(step, ()):
                    gather_far(other)

        begin = jnp.where(p == 5, 4, p)
        end = jnp.where(p == 4, 4, p + 1)
        lax.fori_loop(begin, end, lambda i, c: (five_tiles(i), c)[1], 0)
        return carry

    lax.fori_loop(0, HALF, work, 0)
    lax.fori_loop(HALF, MOST, lambda h, c: (five_tiles(h, True), c)[1], 0)

    for j in range(BLOCKS):
        for d in range(2):
            third(d, j).wait_recv()
        take_back(12 + j)
        take_back(8 + j)

    for d in range(2):
        for g in range(GROUPS):
            first(d, g).wait_send()
        for s in range(HALF):
            second(d, s).wait_send()
        for j in range(BLOCKS):
            third(d, j).wait_send()


def write_out(done, att_ref, gq_ref, gk_ref, gv_ref, out_sem):
    copies = [
        pltpu.make_async_copy(done.at[a], ref, out_sem.at[a])
        for a, ref in enumerate((att_ref, gq_ref, gk_ref, gv_ref))
    ]
    for copy in copies:
        copy.start()
    for copy in copies:
        copy.wait()


def solution(mesh):
    n_dp, n_ctx = mesh.shape["dp"], mesh.shape["ctx"]
    token_spec = P(("dp", "ctx"), None)

    def body(queries, keys, values, grad_out, doc_ids, tile_pairs):
        width = queries.shape[1]
        in_hbm = pl.BlockSpec(memory_space=pltpu.HBM)
        low = jnp.bfloat16
        sem = pltpu.SemaphoreType.DMA
        held = [
            pltpu.with_memory_space_constraint(x, pltpu.HBM)
            for x in (queries, keys, values, grad_out, doc_ids.reshape(-1, TILE), tile_pairs.T)
        ]
        done = pl.pallas_call(
            functools.partial(kernel, n_dp, n_ctx),
            out_shape=jax.ShapeDtypeStruct((4, TILE, width), low),
            in_specs=[in_hbm] * 6,
            out_specs=pl.BlockSpec(memory_space=pltpu.VMEM),
            scratch_shapes=[
                pltpu.VMEM((4, TILE, width), low),
                pltpu.VMEM((2, 4, TILE, width), low),
                pltpu.VMEM((2, 4, TILE, HALF * HEAD), low),
                pltpu.VMEM((2, 4, TILE, MOST * HEAD), low),
                pltpu.VMEM((4, TILE, HALF * HEAD), low),
                pltpu.VMEM((2, 4, TILE, BLOCKS * HEAD), low),
                pltpu.VMEM((2, 4, TILE, BLOCKS * HEAD), low),
                pltpu.VMEM((3 * TILE, 3 * TILE), jnp.float32),
                pltpu.VMEM((2 * TILE, 2 * TILE), jnp.float32),
                pltpu.VMEM((2 * TILE, 2 * TILE), jnp.float32),
                pltpu.VMEM((TILE, TILE), low),
                pltpu.VMEM((2, TILE, TILE), jnp.float32),
                pltpu.VMEM((doc_ids.shape[0] // TILE, TILE), jnp.int32),
                pltpu.VMEM((2, tile_pairs.shape[0]), jnp.int32),
                sem((4,)),
                sem((2,)),
                sem((2, GROUPS)),
                sem((2, GROUPS)),
                sem((2, HALF)),
                sem((2, HALF)),
                sem((2, BLOCKS)),
                sem((2, BLOCKS)),
            ],
            compiler_params=pltpu.CompilerParams(
                collective_id=0, has_side_effects=True, vmem_limit_bytes=48 * 1024 * 1024
            ),
        )(*held)
        shape = jax.ShapeDtypeStruct(queries.shape, low)
        return pl.pallas_call(
            write_out,
            out_shape=(shape,) * 4,
            in_specs=[pl.BlockSpec(memory_space=pl.ANY)],
            out_specs=(in_hbm,) * 4,
            scratch_shapes=[sem((4,))],
            compiler_params=pltpu.CompilerParams(vmem_limit_bytes=1024 * 1024),
        )(done)

    return jax.shard_map(
        body,
        mesh=mesh,
        in_specs=(token_spec,) * 4 + (P(), P()),
        out_specs=(token_spec,) * 4,
        check_vma=False,
    )
```

```python
import functools
import math

import jax
import jax.numpy as jnp
from jax import lax
from jax.experimental import pallas as pl
from jax.experimental.pallas import tpu as pltpu
from jax.sharding import PartitionSpec as P

HEAD = 128
TILE = 128
HEADS = 16
HALF = 8
PER = 2
GROUPS = HALF // PER
WIDE = PER * HEAD
BLOCKS = 4
MOST = 12
GRAIN = 16
GRAINS = TILE // GRAIN
PLANS = (8, 10, 11, 12)
PIECE = {8: 8, 10: 4, 11: 3, 12: 2}
ORDER = {8: (12, 11, 10, 9, 8, 13, 14, 15), 10: (12, 11, 10, 13, 15), 11: (12, 11, 13, 15, 14), 12: (12, 13, 15)}
SCALE = 1.0 / math.sqrt(HEAD)
LOG2E = math.log2(math.e)
FAR = -1e30
MESH_ID = pl.DeviceIdType.MESH


def dot_nt(a, b):
    return lax.dot_general(a, b, (((1,), (1,)), ((), ())), preferred_element_type=jnp.float32)


def dot_nn(a, b):
    return lax.dot_general(a, b, (((1,), (0,)), ((), ())), preferred_element_type=jnp.float32)


def dot_tn(a, b):
    return lax.dot_general(a, b, (((0,), (0,)), ((), ())), preferred_element_type=jnp.float32)


def columns(start, size):
    return pl.ds(pl.multiple_of(start, HEAD), size)


def head_cols(h):
    return slice(h * HEAD, (h + 1) * HEAD)


def grain_rows(start, count):
    return slice(start * GRAIN, (start + count) * GRAIN)


def piece_grain(d, plan, t):
    return GRAINS - PIECE[plan] + t if d == 0 else t


def piece_place(plan, h, t):
    place = h * PIECE[plan] + t
    return ORDER[plan][place // GRAINS], place % GRAINS


def relay_source(d, plan, slot, grain):
    if slot not in ORDER[plan]:
        return None
    place = ORDER[plan].index(slot) * GRAINS + grain
    h, t = place // PIECE[plan], place % PIECE[plan]
    return (h, piece_grain(d, plan, t)) if h < plan else None


def relay_target(d, plan, h, grain):
    if h >= plan:
        return None
    t = grain - piece_grain(d, plan, 0)
    return piece_place(plan, h, t) if 0 <= t < PIECE[plan] else None


def result_place(plan, h, grain):
    if h >= 12:
        return (h - 12, grain)
    if plan == 8 and grain < 4:
        return (h - 8, grain + 4)
    if plan == 10 and h >= 10 and grain < 5:
        return (2 * (h - 10) + grain // 3, 5 + grain % 3)
    if plan == 11 and h == 11 and grain < 6:
        return (grain // 2, 6 + grain % 2)
    return None


def result_source(plan, block, grain):
    for h in range(8, 12):
        for g in range(GRAINS):
            if result_place(plan, h, g) == (block, grain):
                return (h, g)
    return None


def mirrored(d, grain):
    return grain if d == 0 else GRAINS - 1 - grain


def mirrored_pair(d, pair):
    return None if pair is None else (pair[0], mirrored(d, pair[1]))


def runs(entries):
    start = 0
    for at in range(1, GRAINS + 1):
        joined = at < GRAINS and all(
            (a is None and b is None) or (a is not None and b is not None and a[0] == b[0] and b[1] == a[1] + 1)
            for a, b in zip(entries[at - 1], entries[at])
        )
        if not joined:
            yield start, at - start, entries[start]
            start = at


def kernel(
    n_dp, n_ctx,
    q_ref, k_ref, v_ref, g_ref, ids_hbm, pairs_hbm,
    done,
    own, near, stage, far, result, pack, late, mask_wide, mask_left, mask_right, from_right, row_kind, ids_ref, pairs_ref,
    own_sem, side_sem, e1_send, e1_recv, e2_send, e2_recv, late_send, late_recv,
):
    n = n_dp * n_ctx
    me = lax.axis_index("dp") * n_ctx + lax.axis_index("ctx")
    right = lax.rem(me + 1, n)
    left = lax.rem(me + n - 1, n)
    target = [(x // n_ctx, lax.rem(x, n_ctx)) for x in (right, left)]
    inputs = (q_ref, k_ref, v_ref, g_ref)

    def own_copy(a):
        return pltpu.make_async_copy(inputs[a], own.at[a], own_sem.at[a])

    side_copies = [
        pltpu.make_async_copy(ids_hbm, ids_ref, side_sem.at[0]),
        pltpu.make_async_copy(pairs_hbm, pairs_ref, side_sem.at[1]),
    ]

    def first(d, g):
        cols = columns(g * WIDE, WIDE)
        return pltpu.make_async_remote_copy(
            src_ref=own.at[:, :, cols], dst_ref=near.at[d, :, :, cols],
            send_sem=e1_send.at[d, g], recv_sem=e1_recv.at[d, g],
            device_id=target[d], device_id_type=MESH_ID,
        )

    def second(d, s):
        return pltpu.make_async_remote_copy(
            src_ref=stage.at[d, :, :, columns(s * HEAD, HEAD)],
            dst_ref=near.at[d, :, :, columns((HALF + s) * HEAD, HEAD)],
            send_sem=e2_send.at[d, s], recv_sem=e2_recv.at[d, s],
            device_id=target[d], device_id_type=MESH_ID,
        )

    def third(d, j):
        cols = columns(j * HEAD, HEAD)
        return pltpu.make_async_remote_copy(
            src_ref=pack.at[d, :, :, cols], dst_ref=late.at[d, :, :, cols],
            send_sem=late_send.at[d, j], recv_sem=late_recv.at[d, j],
            device_id=target[d], device_id_type=MESH_ID,
        )

    barrier = pltpu.get_barrier_semaphore()
    for d in range(2):
        pl.semaphore_signal(barrier, inc=1, device_id=target[d], device_id_type=MESH_ID)
    for copy in side_copies:
        copy.start()
    for a in range(4):
        own_copy(a).start()
    pl.semaphore_wait(barrier, 2)
    for a in range(4):
        own_copy(a).wait()
    for g in range(GROUPS):
        for d in range(2):
            first(d, g).start()

    for copy in side_copies:
        copy.wait()
    tiles = [lax.rem(me + n + t, n) for t in range(-2, 3)]
    rows = [ids_ref[pl.ds(t, 1), :].astype(jnp.float32) for t in tiles]
    eye = lax.broadcasted_iota(jnp.int32, (TILE, TILE), 0) == lax.broadcasted_iota(jnp.int32, (TILE, TILE), 1)

    def upright(row):
        return jnp.sum(jnp.where(eye, jnp.broadcast_to(row, (TILE, TILE)), 0.0), axis=1, keepdims=True)

    def middle(t):
        before = rows[t - 1][:, TILE - 1 :]
        head, tail = rows[t][:, :1], rows[t][:, TILE - 1 :]
        after = rows[t + 1][:, :1]
        return (before == head) & (head == tail) & (tail == after)

    def plans_of(middle_tile, far_tile):
        count = jnp.sum(jnp.where(rows[far_tile] == rows[middle_tile][:, :1], 1.0, 0.0), axis=1, keepdims=True)
        return {12: count < 33, 11: (count > 32) & (count < 49), 10: (count > 48) & (count < 65), 8: count > 64}

    mid_left, mid_own, mid_right = middle(1), middle(2), middle(3)
    send_plan = [{p: c & mid_own for p, c in plans_of(2, f).items()} for f in (1, 3)]
    recv_plan = [plans_of(1, 0), plans_of(3, 4)]
    codes = pairs_ref[0:1, :] * n + pairs_ref[1:2, :]

    def is_listed(x, y):
        hit = (codes == tiles[x] * n + tiles[y]) | (codes == tiles[y] * n + tiles[x])
        return jnp.max(jnp.where(hit, 1.0, 0.0), axis=1, keepdims=True)

    up = [upright(r) for r in rows]
    flags = {}
    for x in range(5):
        for y in range(x, min(x + 3, 5)):
            flags[x, y] = is_listed(x, y)
            flags[y, x] = flags[x, y]

    def number(condition):
        return jnp.where(condition, 1.0, 0.0)

    def plain(x):
        return rows[x], up[x], [(x, None, None)]

    def mixed(x, y, along, across):
        return (
            jnp.where(along > 0.5, rows[x], rows[y]),
            jnp.where(across > 0.5, up[x], up[y]),
            [(x, along, across), (y, 1.0 - along, 1.0 - across)],
        )

    def mask_of(query_tile, key_tile, keep=None):
        listed = jnp.zeros((TILE, TILE), jnp.float32)
        for x, _, across in query_tile[2]:
            for y, along, _ in key_tile[2]:
                if (x, y) in flags:
                    share = jnp.broadcast_to(flags[x, y], (TILE, TILE))
                    share = share if across is None else share * across
                    listed += share if along is None else share * along
        if keep is not None:
            listed = listed * keep
        return jnp.where((query_tile[1] == key_tile[0]) & (listed > 0.5), 0.0, FAR)

    far_left = [number((r[0] == rows[1][:, :1]) & mid_left) for r in (rows, up)]
    far_right = [number((r[4] == rows[3][:, :1]) & mid_right) for r in (rows, up)]
    take_right = [number((r[1] != rows[2][:, :1]) & mid_own) for r in (rows, up)]
    far_rows = (far_left[1], far_right[1])
    centre = plain(2)
    after = plain(3)
    near_side = mixed(3, 1, *take_right)
    left_side = mixed(0, 2, *far_left)
    right_side = mixed(4, 2, *far_right)
    one, two, three = slice(0, TILE), slice(TILE, 2 * TILE), slice(2 * TILE, 3 * TILE)
    not_middle = 1.0 - number(mid_own)
    mask_wide[one, one] = mask_of(near_side, near_side)
    mask_wide[one, two] = mask_of(near_side, centre)
    mask_wide[two, one] = mask_of(centre, near_side)
    mask_wide[two, two] = mask_of(centre, centre)
    mask_wide[two, three] = mask_of(centre, after, not_middle)
    mask_wide[three, two] = mask_of(after, centre, not_middle)
    mask_wide[three, three] = mask_of(after, after)
    for ref, x, y in ((mask_left, left_side, near_side), (mask_right, right_side, after)):
        ref[one, one] = mask_of(x, x)
        ref[one, two] = mask_of(x, y)
        ref[two, one] = mask_of(y, x)
        ref[two, two] = mask_of(y, y)
    square = (TILE, TILE)
    from_right[...] = jnp.broadcast_to(take_right[1], square).astype(jnp.bfloat16)
    reaches_left = number(up[2] == rows[1][:, TILE - 1 :])
    reaches_right = number(up[2] == rows[3][:, :1])
    row_kind[0] = jnp.broadcast_to(reaches_left, square)
    row_kind[1] = jnp.broadcast_to(reaches_right, square)
    returned = [reaches_left * number(mid_left), reaches_right * number(mid_right)]

    def pass_on(slot):
        for d in range(2):
            entries = [
                [(slot, grain)] + [relay_source(d, plan, slot, grain) for plan in PLANS] for grain in range(GRAINS)
            ]
            for start, count, sources in runs(entries):
                value = own[:, grain_rows(start, count), head_cols(slot)]
                for plan, source in zip(PLANS, sources[1:]):
                    if source is not None:
                        other = near[d, :, grain_rows(source[1], count), head_cols(source[0])]
                        value = jnp.where(send_plan[d][plan], other, value)
                stage[d, :, grain_rows(start, count), head_cols(slot - HALF)] = value
            second(d, slot - HALF).start()

    def gather_far(h):
        for d in range(2):
            entries = [
                [relay_target(d, plan, h, grain) or (None if plan != 8 else (8, grain)) for plan in PLANS]
                for grain in range(GRAINS)
            ]
            for start, count, sources in runs(entries):
                value = None
                for plan, source in zip(PLANS, sources):
                    if source is not None:
                        other = near[d, :, grain_rows(source[1], count), head_cols(source[0])]
                        value = other if value is None else jnp.where(recv_plan[d][plan], other, value)
                r = grain_rows(start, count)
                for a in range(4):
                    far[d, a, r, head_cols(h)] = jnp.where(far_rows[d][r] > 0.5, value[a], own[a, r, head_cols(h)])

    def softmax_parts(query, grads, keys, values, mask):
        scores = dot_nt(query, keys) * (SCALE * LOG2E) + mask
        top = jnp.max(scores, axis=1, keepdims=True)
        weights = jnp.exp2(scores - top)
        inverse = 1.0 / jnp.sum(weights, axis=1, keepdims=True)
        dprobs = dot_nt(grads, values)
        delta = jnp.sum(weights * dprobs, axis=1, keepdims=True) * inverse
        return weights, inverse, dprobs, delta

    def load(h):
        at = columns(h * HEAD, HEAD)
        after_rows = [near[1, a, :, at] for a in range(4)]
        use_right = from_right[...] > 0.5
        near_rows = [jnp.where(use_right, after_rows[a], near[0, a, :, at]) for a in range(4)]
        return at, near_rows, [own[a, :, at] for a in range(4)], after_rows

    def stacked(*parts):
        return [jnp.concatenate(part, axis=0) for part in zip(*parts)]

    def full(parts):
        weights, inverse, dprobs, delta = parts
        p = weights * inverse
        return p.astype(jnp.bfloat16), (p * (dprobs - delta)).astype(jnp.bfloat16)

    def partial(parts, cols):
        weights, inverse, dprobs, delta = parts
        p = weights[:, cols] * inverse
        return p.astype(jnp.bfloat16), (p * (dprobs[:, cols] - delta)).astype(jnp.bfloat16)

    def three_tiles(h):
        at, near_rows, own_rows, after_rows = load(h)
        back = columns((h - HALF) * HEAD, HEAD)
        q, k, v, g = stacked(near_rows, own_rows, after_rows)
        wide = slice(0, 2 * TILE)
        p_near, ds_near = full(softmax_parts(q[one], g[one], k[wide], v[wide], mask_wide[one, wide]))
        p_own, ds_own = full(softmax_parts(q[two], g[two], k, v, mask_wide[two, :]))
        tail = slice(TILE, 3 * TILE)
        p_after, ds_after = partial(softmax_parts(q[three], g[three], k[tail], v[tail], mask_wide[three, tail]), one)
        result[0, :, back] = dot_nn(p_near, v[wide]).astype(jnp.bfloat16)
        result[1, :, back] = (dot_nn(ds_near, k[wide]) * SCALE).astype(jnp.bfloat16)
        result[2, :, back] = (
            dot_tn(jnp.concatenate([ds_near[:, one], ds_own[:, one]], axis=0), q[wide]) * SCALE
        ).astype(jnp.bfloat16)
        result[3, :, back] = dot_tn(
            jnp.concatenate([p_near[:, one], p_own[:, one]], axis=0), g[wide]
        ).astype(jnp.bfloat16)
        done[0, :, at] = dot_nn(p_own, v).astype(jnp.bfloat16)
        done[1, :, at] = (dot_nn(ds_own, k) * SCALE).astype(jnp.bfloat16)
        done[2, :, at] = (
            dot_tn(jnp.concatenate([ds_near[:, two], ds_own[:, two], ds_after], axis=0), q) * SCALE
        ).astype(jnp.bfloat16)
        done[3, :, at] = dot_tn(
            jnp.concatenate([p_near[:, two], p_own[:, two], p_after], axis=0), g
        ).astype(jnp.bfloat16)

    def two_tiles(first_rows, second_rows, mask):
        q, k, v, g = stacked(first_rows, second_rows)
        p_one, ds_one = full(softmax_parts(q[one], g[one], k, v, mask[one, :]))
        p_two, ds_two = partial(softmax_parts(q[two], g[two], k, v, mask[two, :]), one)
        return (
            dot_nn(p_one, v),
            dot_nn(ds_one, k) * SCALE,
            dot_tn(jnp.concatenate([ds_one[:, one], ds_two], axis=0), q) * SCALE,
            dot_tn(jnp.concatenate([p_one[:, one], p_two], axis=0), g),
        )

    def five_tiles(h, known=False):
        at, near_rows, own_rows, after_rows = load(h)
        far_sides = [[far[d, a, :, at] for a in range(4)] for d in range(2)]
        before = two_tiles(far_sides[0], near_rows, mask_left)
        behind = two_tiles(far_sides[1], after_rows, mask_right)
        if known:
            inside = [done[a, :, at].astype(jnp.float32) for a in range(4)]
        else:
            q, k, v, g = own_rows
            p, ds = full(softmax_parts(q, g, k, v, mask_wide[two, two]))
            inside = (dot_nn(p, v), dot_nn(ds, k) * SCALE, dot_tn(ds, q) * SCALE, dot_tn(p, g))
        on_left, on_right = row_kind[0] > 0.5, row_kind[1] > 0.5
        for a in range(4):
            value = jnp.where(on_left, before[a], jnp.where(on_right, behind[a], inside[a]))
            done[a, :, at] = value.astype(jnp.bfloat16)

    def send_back(j):
        for d in range(2):
            entries = [
                [(12 + j, grain)]
                + [mirrored_pair(d, result_source(plan, j, mirrored(d, grain))) for plan in PLANS]
                for grain in range(GRAINS)
            ]
            for start, count, sources in runs(entries):
                value = result[:, grain_rows(start, count), head_cols(4 + j)]
                for plan, source in zip(PLANS, sources[1:]):
                    if source is not None:
                        other = result[:, grain_rows(source[1], count), head_cols(source[0] - HALF)]
                        value = jnp.where(send_plan[d][plan], other, value)
                pack[d, :, grain_rows(start, count), head_cols(j)] = value
            third(d, j).start()

    def take_back(h):
        for d in range(2):
            entries = [
                [mirrored_pair(d, result_place(plan, h, mirrored(d, grain))) for plan in PLANS]
                for grain in range(GRAINS)
            ]
            for start, count, sources in runs(entries):
                r = grain_rows(start, count)
                for plan, source in zip(PLANS, sources):
                    if source is None or (h >= 12 and plan != 8):
                        continue
                    take = returned[d][r] > 0.5
                    if h < 12:
                        take = take & recv_plan[d][plan]
                    for a in range(4):
                        other = late[d, a, grain_rows(source[1], count), head_cols(source[0])]
                        done[a, r, head_cols(h)] = jnp.where(take, other, done[a, r, head_cols(h)])

    early_slots = ((), (12,), (11, 10, 9, 8), (13,))
    for g in range(GROUPS):
        for d in range(2):
            first(d, g).wait_recv()
        for slot in early_slots[g]:
            pass_on(slot)

    complete = {4: 0, 5: 1, 6: 2, 7: 3}
    ready = {0: (0,), 1: (1,), 2: (2,), 3: (3,), 5: (4, 5), 6: (6,), 7: (7, 8, 9, 10, 11)}

    def work(p, carry):
        h = jnp.where(p < 5, 12 - p, 8 + p)
        for d in range(2):
            second(d, h - HALF).wait_recv()

        @pl.when(p == 2)
        def _():
            pass_on(14)

        @pl.when(p == 4)
        def _():
            pass_on(15)

        three_tiles(h)
        for step in range(HALF):

            @pl.when(p == step)
            def _():
                if step in complete:
                    send_back(complete[step])
                for other in ready.get(step, ()):
                    gather_far(other)

        begin = jnp.where(p == 5, 4, p)
        end = jnp.where(p == 4, 4, p + 1)
        lax.fori_loop(begin, end, lambda i, c: (five_tiles(i), c)[1], 0)
        return carry

    lax.fori_loop(0, HALF, work, 0)
    lax.fori_loop(HALF, MOST, lambda h, c: (five_tiles(h, True), c)[1], 0)

    for j in range(BLOCKS):
        for d in range(2):
            third(d, j).wait_recv()
        take_back(12 + j)
        take_back(8 + j)

    for d in range(2):
        for g in range(GROUPS):
            first(d, g).wait_send()
        for s in range(HALF):
            second(d, s).wait_send()
        for j in range(BLOCKS):
            third(d, j).wait_send()


def write_out(done, att_ref, gq_ref, gk_ref, gv_ref, out_sem):
    half = TILE // 2
    copies = [
        pltpu.make_async_copy(done.at[a, pl.ds(b * half, half)], ref.at[pl.ds(b * half, half)], out_sem.at[a, b])
        for b in range(2)
        for a, ref in enumerate((att_ref, gq_ref, gk_ref, gv_ref))
    ]
    for copy in copies:
        copy.start()
    for copy in copies:
        copy.wait()


def solution(mesh):
    n_dp, n_ctx = mesh.shape["dp"], mesh.shape["ctx"]
    token_spec = P(("dp", "ctx"), None)

    def body(queries, keys, values, grad_out, doc_ids, tile_pairs):
        width = queries.shape[1]
        in_hbm = pl.BlockSpec(memory_space=pltpu.HBM)
        low = jnp.bfloat16
        sem = pltpu.SemaphoreType.DMA
        held = [
            pltpu.with_memory_space_constraint(x, pltpu.HBM)
            for x in (queries, keys, values, grad_out, doc_ids.reshape(-1, TILE), tile_pairs.T)
        ]
        done = pl.pallas_call(
            functools.partial(kernel, n_dp, n_ctx),
            out_shape=jax.ShapeDtypeStruct((4, TILE, width), low),
            in_specs=[in_hbm] * 6,
            out_specs=pl.BlockSpec(memory_space=pltpu.VMEM),
            scratch_shapes=[
                pltpu.VMEM((4, TILE, width), low),
                pltpu.VMEM((2, 4, TILE, width), low),
                pltpu.VMEM((2, 4, TILE, HALF * HEAD), low),
                pltpu.VMEM((2, 4, TILE, MOST * HEAD), low),
                pltpu.VMEM((4, TILE, HALF * HEAD), low),
                pltpu.VMEM((2, 4, TILE, BLOCKS * HEAD), low),
                pltpu.VMEM((2, 4, TILE, BLOCKS * HEAD), low),
                pltpu.VMEM((3 * TILE, 3 * TILE), jnp.float32),
                pltpu.VMEM((2 * TILE, 2 * TILE), jnp.float32),
                pltpu.VMEM((2 * TILE, 2 * TILE), jnp.float32),
                pltpu.VMEM((TILE, TILE), low),
                pltpu.VMEM((2, TILE, TILE), jnp.float32),
                pltpu.VMEM((doc_ids.shape[0] // TILE, TILE), jnp.int32),
                pltpu.VMEM((2, tile_pairs.shape[0]), jnp.int32),
                sem((4,)),
                sem((2,)),
                sem((2, GROUPS)),
                sem((2, GROUPS)),
                sem((2, HALF)),
                sem((2, HALF)),
                sem((2, BLOCKS)),
                sem((2, BLOCKS)),
            ],
            compiler_params=pltpu.CompilerParams(
                collective_id=0, has_side_effects=True, vmem_limit_bytes=48 * 1024 * 1024
            ),
        )(*held)
        shape = jax.ShapeDtypeStruct(queries.shape, low)
        return pl.pallas_call(
            write_out,
            out_shape=(shape,) * 4,
            in_specs=[pl.BlockSpec(memory_space=pl.ANY)],
            out_specs=(in_hbm,) * 4,
            scratch_shapes=[sem((4, 2))],
            compiler_params=pltpu.CompilerParams(vmem_limit_bytes=1024 * 1024),
        )(done)

    return jax.shard_map(
        body,
        mesh=mesh,
        in_specs=(token_spec,) * 4 + (P(), P()),
        out_specs=(token_spec,) * 4,
        check_vma=False,
    )
```
